256 devices in a mesh: dp: 64 (over z, y, core), tensor: 4 (over x).
Axes of the slice: x: 4, y: 4, z: 8, core: 2. Of those that a mesh axis runs over, the one named last changes fastest.
Arguments:
- inputs: bfloat16 [8192, 8192], P('dp', 'tensor'), may hold values from -6 to 6
- cotangent: bfloat16 [8192, 1024], P('dp', 'tensor'), may hold values from -6 to 6
- frozen_key_weight: bfloat16 [8192, 1024], P(None, 'tensor'), may hold values from -0.1875 to 0.1875
- adapter_down_weight: bfloat16 [64, 16, 8192], P('dp', None, 'tensor'), may hold values from -0.0625 to 0.0625
- adapter_up_weight: bfloat16 [64, 16, 1024], P('dp', None, 'tensor'), may hold values from -0.1875 to 0.1875
- tenant_per_block: int32 [64], P('dp'), may hold values from 0 to 63
Outputs:
- grad_inputs: bfloat16 [8192, 8192], P('dp', 'tensor')
- grad_down: float32 [64, 16, 8192], P('dp', None, 'tensor')
- grad_up: float32 [64, 16, 1024], P('dp', None, 'tensor')
The draws below stay inside these ranges and needn't reach their ends.
All inputs are finite; a program needn't handle non-finite values.
Results may differ from the reference program's by a relative error of at most 0.0034.
Values may be sent and summed in bfloat16 or wider, within the bound.
A program may use at most 128 MiB of HBM per device.

```python
import math
import jax
import jax.numpy as jnp
import numpy as np
from jax import lax

MODEL_WIDTH = 8192
KEY_WIDTH = 1024
ADAPTER_RANK = 16
BLOCK_ROWS = 128
TENANT_TOTAL = 64
TOKENS = 8192
BLOCKS = 64


def touch_ends(entries, stream_key, least, top_value):
    shape = entries.shape
    place = [jax.random.randint(jax.random.fold_in(stream_key, axis), (), 0, shape[axis]) for axis in range(len(shape))]
    entries = entries.at[tuple(place)].set(least)
    longest = shape.index(max(shape))
    place[longest] = (place[longest] + 1) % shape[longest]
    return entries.at[tuple(place)].set(top_value)


def shard_levels(rng, shape, split, low, high):
    level, own = 1.0, jax.random.fold_in(rng, 6)
    for dim, shards_of in split:
        heights = jnp.exp(jax.random.uniform(jax.random.fold_in(own, dim), (shards_of,), jnp.float32, low / len(split), high / len(split)))
        level = level * jnp.repeat(heights, shape[dim] // shards_of).reshape([-1 if axis == dim else 1 for axis in range(len(shape))])
    return level


def cumulative_ranks(number_of, skew):
    portions = [(1 << 20) // math.isqrt(rank ** skew) + 1 for rank in range(1, number_of + 1)]
    scale = 1 + sum(portions) // (1 << 30)
    return np.cumsum(np.array([max(1, weight // scale) for weight in portions]))


def skewed_ids(key, extent, amount, lean):
    grid = cumulative_ranks(amount, lean)
    ticket = jax.random.randint(jax.random.fold_in(key, 1), extent, 0, int(grid[amount - 1]))
    standing = jnp.searchsorted(jnp.asarray(grid, jnp.int32), ticket, side="right")
    return jax.random.permutation(jax.random.fold_in(key, 2), amount)[standing].astype(jnp.int32)


def noise(stream_key, shape, scale, limit, split=(), held_as=jnp.bfloat16):
    array = jax.random.normal(stream_key, shape, jnp.float32) * scale
    if len(split) > 0:
        array = shard_levels(stream_key, shape, split, -0.22, 0.18) * array
    return jnp.clip(array, min=-limit, max=limit).astype(held_as)


def setup_inputs(seed: int = 0) -> dict:
    splits = jax.random.split(jax.random.key(seed), 7)
    inputs = noise(splits[0], (TOKENS, MODEL_WIDTH), 1.0, 6.0, ((0, 64), (1, 4)))
    cotangent = noise(splits[1], (TOKENS, KEY_WIDTH), 1.0, 6.0, ((0, 64), (1, 4)))
    frozen_key_weight = noise(splits[2], (MODEL_WIDTH, KEY_WIDTH), KEY_WIDTH ** -0.5, 0.1875, ((1, 4),))
    adapter_down_weight = noise(splits[3], (TENANT_TOTAL, ADAPTER_RANK, MODEL_WIDTH), MODEL_WIDTH ** -0.5, 0.0625, ((0, 64), (2, 4)))
    adapter_up_weight = noise(splits[4], (TENANT_TOTAL, ADAPTER_RANK, KEY_WIDTH), KEY_WIDTH ** -0.5, 0.1875, ((0, 64), (2, 4)))
    tenant_per_block = touch_ends(skewed_ids(splits[5], (BLOCKS,), TENANT_TOTAL, 2), jax.random.fold_in(splits[5], 3), 0, TENANT_TOTAL - 1).astype(jnp.int32)
    return dict(inputs=inputs, cotangent=cotangent, frozen_key_weight=frozen_key_weight, adapter_down_weight=adapter_down_weight, adapter_up_weight=adapter_up_weight, tenant_per_block=tenant_per_block)


ADAPTER_SCALE = 2.0


def reference(inputs, cotangent, frozen_key_weight, adapter_down_weight, adapter_up_weight, tenant_per_block):
    input_blocks = inputs.reshape(BLOCKS, BLOCK_ROWS, MODEL_WIDTH)
    cotangent_blocks = cotangent.reshape(BLOCKS, BLOCK_ROWS, KEY_WIDTH)

    def per_block(item):
        x_rows, gradient_rows, current_tenant = item
        down_matrix = lax.dynamic_index_in_dim(adapter_down_weight, current_tenant.astype(jnp.int32), 0, keepdims=False)
        up_matrix = lax.dynamic_index_in_dim(adapter_up_weight, current_tenant.astype(jnp.int32), 0, keepdims=False)
        low_in = jnp.dot(x_rows, down_matrix.T, preferred_element_type=jnp.float32)
        reduced_output = ADAPTER_SCALE * jnp.dot(gradient_rows, up_matrix.T, preferred_element_type=jnp.float32)
        reduced_input_batch = low_in.astype(jnp.bfloat16)
        low_out_b = reduced_output.astype(jnp.bfloat16)
        grad_rows = jnp.dot(gradient_rows, frozen_key_weight.T, preferred_element_type=jnp.float32)
        grad_rows = grad_rows + jnp.dot(low_out_b, down_matrix, preferred_element_type=jnp.float32)
        down_term = jnp.dot(low_out_b.T, x_rows, preferred_element_type=jnp.float32)
        up_partial_product = ADAPTER_SCALE * jnp.dot(reduced_input_batch.T, gradient_rows, preferred_element_type=jnp.float32)
        return grad_rows.astype(jnp.bfloat16), down_term, up_partial_product

    grad_blocks, down_terms, up_terms = lax.map(per_block, (input_blocks, cotangent_blocks, tenant_per_block))
    grad_inputs = grad_blocks.reshape(TOKENS, MODEL_WIDTH)
    grad_down = jax.ops.segment_sum(down_terms, tenant_per_block, num_segments=TENANT_TOTAL)
    grad_up = jax.ops.segment_sum(up_terms, tenant_per_block, num_segments=TENANT_TOTAL)
    return grad_inputs, grad_down, grad_up
```

```python
import jax
import jax.numpy as jnp
from jax import lax
from jax.experimental import pallas as pl
from jax.experimental.pallas import tpu as pltpu
from jax.sharding import PartitionSpec as P

MESH = pl.DeviceIdType.MESH
F32 = jnp.float32
BF16 = jnp.bfloat16
ADAPTER_SCALE = 2.0

Z, Y, CORES, X = 8, 4, 2, 4
G = Z * CORES
ROWS, WIDTH, KEYS, RANK, LANES = 128, 2048, 256, 16, 128
TABLE = G * RANK + 2 * RANK


def dot(a, b, dims=((1,), (0,))):
    return lax.dot_general(a, b, (dims, ((), ())), preferred_element_type=F32)


def kernel(
    inputs_hbm, cot_ref, weight_hbm, down_ref, up_ref, tenant_ref,
    out_hbm, grad_down_ref, grad_up_ref,
    xs, weight, partial, own, arrived, out_vm, cot_spread, pick,
    s1, r1, r2, s3, r3, r4, s5, r5, s6, r6, s7, r7,
    load_sem, store_sem, send_sem, recv_sem, xsend_sem, xrecv_sem,
):
    me, mx = lax.axis_index("dp"), lax.axis_index("tensor")
    z, y, c = lax.div(me, Y * CORES), lax.rem(lax.div(me, CORES), Y), lax.rem(me, CORES)
    g = z * CORES + c

    def group_member(i):
        h = lax.rem(g + G // 2 + (1 - 2 * lax.rem(i, 2)) * lax.div(i + 1, 2), G)
        return h, (lax.div(h, CORES) * Y + y) * CORES + lax.rem(h, CORES)

    def y_member(k):
        h = lax.rem(y + k, Y)
        return h, (z * Y + h) * CORES + c

    load_weight = pltpu.make_async_copy(weight_hbm, weight, load_sem.at[0])
    load_inputs = pltpu.make_async_copy(inputs_hbm, xs, load_sem.at[1])

    barrier = pltpu.get_barrier_semaphore()

    @pl.loop(0, G - 1)
    def _(i):
        _, device = group_member(i)
        pl.semaphore_signal(barrier, inc=1, device_id={"dp": device}, device_id_type=MESH)

    for k in (2, 1, 3):
        pl.semaphore_signal(barrier, inc=1, device_id={"dp": y_member(k)[1]}, device_id_type=MESH)
        pl.semaphore_signal(barrier, inc=1, device_id={"tensor": lax.rem(mx + k, X)}, device_id_type=MESH)

    load_weight.start()
    load_inputs.start()

    lane0 = RANK * lax.rem(g, 8)
    key = lax.broadcasted_iota(jnp.int32, (KEYS, KEYS), 0)
    column = lax.broadcasted_iota(jnp.int32, (KEYS, KEYS), 1)
    target = lax.div(key, RANK) * LANES + lax.rem(key, RANK) + lane0
    lane = lax.broadcasted_iota(jnp.int32, (RANK, LANES), 1)
    block_of_lane = lax.div(lane, RANK)
    tenant = jnp.full((RANK, LANES), tenant_ref[0], jnp.int32).astype(F32)
    tenant = jnp.where(block_of_lane == lax.rem(g + 1, 8), tenant, 0.0)
    cot = cot_ref[...]
    up = up_ref[0]
    for i in range(WIDTH // KEYS):
        spread = (column + i * KEYS == target).astype(F32).astype(BF16)
        cot_spread[:, i * KEYS : (i + 1) * KEYS] = dot(cot, spread).astype(BF16)
        up_spread = dot(up, spread)
        for q in range(2):
            tile = up_spread[:, q * LANES : (q + 1) * LANES] + tenant
            s1[2 * i + q, RANK:, :] = tile.astype(BF16)
    for q in range(G):
        s1[q, :RANK, :] = down_ref[0, :, q * LANES : (q + 1) * LANES]

    def group_exchange(step, src, dst):
        @pl.loop(0, G - 1)
        def _(i):
            h, device = group_member(i)
            pltpu.make_async_remote_copy(
                src.at[h], dst.at[g], send_sem.at[step], recv_sem.at[step],
                device_id={"dp": device}, device_id_type=MESH,
            ).start()

        pltpu.make_async_copy(src.at[g], dst.at[g], recv_sem.at[step]).start()

    def received(step, dst):
        pltpu.make_async_copy(dst, dst, recv_sem.at[step]).wait()

    load_weight.wait()
    for k in range(X):
        q = lax.rem(mx + k, X)

        @pl.loop(0, WIDTH // KEYS)
        def _(i):
            at = pl.multiple_of(q * WIDTH + i * KEYS, KEYS)
            product = dot(cot, weight[pl.ds(at, KEYS), :], ((1,), (1,)))
            columns = pl.ds(pl.multiple_of(i * KEYS, KEYS), KEYS)
            if k == 0:
                own[:, columns] = product
            else:
                partial[k - 1, :, columns] = product.astype(BF16)

    load_inputs.wait()
    pl.semaphore_wait(barrier, G - 1 + Y - 1 + X - 1)

    group_exchange(0, s1, r1)
    shares = []
    for k in (2, 1, 3):
        share = pltpu.make_async_remote_copy(
            partial.at[k - 1], arrived.at[k - 1], xsend_sem.at[k - 1], xrecv_sem.at[k - 1],
            device_id={"tensor": lax.rem(mx + k, X)}, device_id_type=MESH,
        )
        share.start()
        shares.append(share)
    received(0, r1)

    mine = r2.at[y]
    packed = [jnp.zeros((RANK, LANES), F32), jnp.zeros((RANK, LANES), F32)]
    for h in range(G):
        mine[h * RANK : (h + 1) * RANK, :] = r1[h, :RANK, :]
        tile = r1[h, RANK:, :].astype(F32)
        packed[h // 8] = jnp.where(block_of_lane == h % 8, tile, packed[h // 8])
    for q in range(2):
        mine[(G + q) * RANK : (G + q + 1) * RANK, :] = packed[q].astype(BF16)
    for k in (2, 1, 3):
        pltpu.make_async_remote_copy(
            mine, mine, send_sem.at[1], recv_sem.at[1],
            device_id={"dp": y_member(k)[1]}, device_id_type=MESH,
        ).start()

    rank_row = lax.broadcasted_iota(jnp.int32, (RANK, 1), 0)
    slot = lax.broadcasted_iota(jnp.int32, (RANK, Y * G * RANK), 1)
    for h in range(G):
        at = RANK * ((h + 1) % 8)
        t = r1[h, RANK:, at : at + 1].astype(F32).astype(jnp.int32)
        t_y, t_g = (t >> 1) & 3, (t >> 3) * 2 + (t & 1)
        wanted = (t_y * G + t_g) * RANK + rank_row
        pick[h * RANK : (h + 1) * RANK, :] = (slot == wanted).astype(F32).astype(BF16)

    def pick_of(q):
        return pick[:, q * KEYS : (q + 1) * KEYS]

    others = r2.at[pl.ds(0, Y - 1)]
    pltpu.make_async_copy(others, others, recv_sem.at[1]).wait()

    down_tiles = jnp.zeros((KEYS, LANES), F32)
    up_tiles = jnp.zeros((RANK, KEYS), F32)
    for q in range(Y):
        down_tiles += dot(pick_of(q), r2[q, : G * RANK, :])
        tiles = jnp.concatenate([r2[q, G * RANK : (G + 1) * RANK, :], r2[q, (G + 1) * RANK :, :]], axis=1)
        up_tiles += dot(tiles, pick_of(q), ((1,), (1,)))
    for h in range(G):
        s3[h, :RANK, :] = down_tiles[h * RANK : (h + 1) * RANK].astype(BF16)
        s3[h, RANK:, :] = up_tiles[:, h // 8 * LANES : (h // 8 + 1) * LANES].astype(BF16)
    group_exchange(2, s3, r3)
    received(2, r3)

    down_b = jnp.concatenate([r3[h, :RANK, :] for h in range(G)], axis=1)
    up_b = jnp.concatenate([r3[h, RANK:, :] for h in range(G)], axis=1)
    r4[mx, :RANK, :] = dot(down_b, xs[...], ((1,), (1,)))
    r4[mx, RANK:, :] = ADAPTER_SCALE * dot(up_b, cot_spread[...], ((1,), (1,)))
    for k in (2, 1, 3):
        pltpu.make_async_remote_copy(
            r4.at[mx], r4.at[mx], send_sem.at[3], recv_sem.at[3],
            device_id={"tensor": lax.rem(mx + k, X)}, device_id_type=MESH,
        ).start()
    others = r4.at[pl.ds(0, X - 1)]
    pltpu.make_async_copy(others, others, recv_sem.at[3]).wait()
    low = ((r4[0] + r4[1]) + (r4[2] + r4[3])).astype(BF16)
    low_in, low_out = low[:RANK], low[RANK:]

    for i in range(WIDTH // KEYS):
        columns = slice(i * KEYS, (i + 1) * KEYS)
        down_term = dot(low_out, xs[:, columns]).astype(BF16)
        up_term = (ADAPTER_SCALE * dot(low_in, cot_spread[:, columns])).astype(BF16)
        for q in range(2):
            s5[2 * i + q, :RANK, :] = down_term[:, q * LANES : (q + 1) * LANES]
            s5[2 * i + q, RANK:, :] = up_term[:, q * LANES : (q + 1) * LANES]
    group_exchange(4, s5, r5)
    for i in range(WIDTH // KEYS):
        columns = slice(i * KEYS, (i + 1) * KEYS)
        own[:, columns] += dot(low_out, down_b[:, columns], ((0,), (0,)))
    received(4, r5)

    down_terms = r5[:, :RANK, :].reshape(G * RANK, LANES)
    packed = []
    for q in range(2):
        total = r5[8 * q, RANK:, :].astype(F32)
        for h in range(8 * q + 1, 8 * q + 8):
            total += r5[h, RANK:, :].astype(F32)
        packed.append(total.astype(BF16))
    up_terms = jnp.concatenate(packed, axis=1)
    for q in range(Y):
        s6[q, : G * RANK, :] = dot(pick_of(q), down_terms, ((0,), (0,))).astype(BF16)
        sums = dot(up_terms, pick_of(q)).astype(BF16)
        s6[q, G * RANK : (G + 1) * RANK, :] = sums[:, :LANES]
        s6[q, (G + 1) * RANK :, :] = sums[:, LANES:]
    for k in (2, 1, 3):
        h, device = y_member(k)
        pltpu.make_async_remote_copy(
            s6.at[h], r6.at[y], send_sem.at[5], recv_sem.at[5],
            device_id={"dp": device}, device_id_type=MESH,
        ).start()
    pltpu.make_async_copy(s6.at[y], r6.at[y], recv_sem.at[5]).start()
    received(5, r6)

    for h in range(G + 2):
        rows = slice(h * RANK, (h + 1) * RANK)
        total = (r6[0, rows, :].astype(F32) + r6[1, rows, :].astype(F32)) + (
            r6[2, rows, :].astype(F32) + r6[3, rows, :].astype(F32)
        )
        if h < G:
            s7[h, :RANK, :] = total
        else:
            for owner in range(8 * (h - G), 8 * (h - G) + 8):
                s7[owner, RANK:, :] = total
    group_exchange(6, s7, r7)

    for share in shares:
        share.wait()
    for i in range(WIDTH // KEYS):
        columns = slice(i * KEYS, (i + 1) * KEYS)
        total = own[:, columns]
        for k in range(X - 1):
            total += arrived[k, :, columns].astype(F32)
        out_vm[:, columns] = total.astype(BF16)
    store_out = pltpu.make_async_copy(out_vm, out_hbm, store_sem)
    store_out.start()
    received(6, r7)

    for h in range(G):
        grad_down_ref[0, :, h * LANES : (h + 1) * LANES] = r7[h, :RANK, :]
    for q in range(2):
        total = jnp.zeros((RANK, LANES), F32)
        for h in range(8 * q, 8 * q + 8):
            moved = pltpu.roll(r7[h, RANK:, :], lax.rem(RANK * (h % 8) + LANES - lane0, LANES), 1)
            total = jnp.where(block_of_lane == h % 8, moved, total)
        grad_up_ref[0, :, q * LANES : (q + 1) * LANES] = total

    store_out.wait()
    for step, sent in ((0, s1), (2, s3), (4, s5), (6, s7)):
        peers = sent.at[pl.ds(0, G - 1)]
        pltpu.make_async_copy(peers, peers, send_sem.at[step]).wait()
    for step, sent in ((1, r2), (3, r4), (5, s6)):
        peers = sent.at[pl.ds(0, 3)]
        pltpu.make_async_copy(peers, peers, send_sem.at[step]).wait()


def on_device(inputs, cotangent, frozen_key_weight, adapter_down_weight, adapter_up_weight, tenant_per_block):
    hbm = pl.BlockSpec(memory_space=pl.ANY)
    vmem = pl.BlockSpec(memory_space=pltpu.VMEM)
    smem = pl.BlockSpec(memory_space=pltpu.SMEM)
    dma = pltpu.SemaphoreType.DMA
    return pl.pallas_call(
        kernel,
        out_shape=(
            jax.ShapeDtypeStruct((ROWS, WIDTH), BF16),
            jax.ShapeDtypeStruct((1, RANK, WIDTH), F32),
            jax.ShapeDtypeStruct((1, RANK, KEYS), F32),
        ),
        in_specs=[hbm, vmem, hbm, vmem, vmem, smem],
        out_specs=(hbm, vmem, vmem),
        scratch_shapes=[
            pltpu.VMEM((ROWS, WIDTH), BF16),
            pltpu.VMEM((X * WIDTH, KEYS), BF16),
            pltpu.VMEM((X - 1, ROWS, WIDTH), BF16),
            pltpu.VMEM((ROWS, WIDTH), F32),
            pltpu.VMEM((X - 1, ROWS, WIDTH), BF16),
            pltpu.VMEM((ROWS, WIDTH), BF16),
            pltpu.VMEM((ROWS, WIDTH), BF16),
            pltpu.VMEM((G * RANK, Y * G * RANK), BF16),
            pltpu.VMEM((G, 2 * RANK, LANES), BF16),
            pltpu.VMEM((G, 2 * RANK, LANES), BF16),
            pltpu.VMEM((Y, TABLE, LANES), BF16),
            pltpu.VMEM((G, 2 * RANK, LANES), BF16),
            pltpu.VMEM((G, 2 * RANK, LANES), BF16),
            pltpu.VMEM((X, 2 * RANK, LANES), F32),
            pltpu.VMEM((G, 2 * RANK, LANES), BF16),
            pltpu.VMEM((G, 2 * RANK, LANES), BF16),
            pltpu.VMEM((Y, TABLE, LANES), BF16),
            pltpu.VMEM((Y, TABLE, LANES), BF16),
            pltpu.VMEM((G, 2 * RANK, LANES), F32),
            pltpu.VMEM((G, 2 * RANK, LANES), F32),
            dma((2,)), dma, dma((7,)), dma((7,)), dma((X - 1,)), dma((X - 1,)),
        ],
        compiler_params=pltpu.CompilerParams(
            collective_id=0, has_side_effects=True, vmem_limit_bytes=40 << 20
        ),
    )(inputs, cotangent, frozen_key_weight, adapter_down_weight, adapter_up_weight, tenant_per_block)


def solution(mesh):
    in_specs = (
        P("dp", "tensor"),
        P("dp", "tensor"),
        P(None, "tensor"),
        P("dp", None, "tensor"),
        P("dp", None, "tensor"),
        P("dp"),
    )
    out_specs = (P("dp", "tensor"), P("dp", None, "tensor"), P("dp", None, "tensor"))
    return jax.shard_map(
        on_device, mesh=mesh, in_specs=in_specs, out_specs=out_specs, check_vma=False
    )
```

```python
import jax
import jax.numpy as jnp
from jax import lax
from jax.experimental import pallas as pl
from jax.experimental.pallas import tpu as pltpu
from jax.sharding import PartitionSpec as P

MESH = pl.DeviceIdType.MESH
F32 = jnp.float32
BF16 = jnp.bfloat16
ADAPTER_SCALE = 2.0

Z, Y, CORES, X = 8, 4, 2, 4
G = Z * CORES
ROWS, WIDTH, KEYS, RANK, LANES = 128, 2048, 256, 16, 128
TABLE = G * RANK + 2 * RANK


def dot(a, b, dims=((1,), (0,))):
    return lax.dot_general(a, b, (dims, ((), ())), preferred_element_type=F32)


def kernel(
    inputs_hbm, cot_hbm, weight_hbm, down_hbm, up_hbm, tenant_ref,
    out_hbm, grad_down_hbm, grad_up_hbm,
    xs, cot_vm, weight, down_vm, up_vm, partial, own, arrived, out_vm, grad_down, grad_up, cot_spread, pick,
    s1, r1, r2, s3, r3, r4, s5, r5, s6, r6, s7, r7,
    load_sem, store_sem, send_sem, recv_sem, xsend_sem, xrecv_sem,
):
    me, mx = lax.axis_index("dp"), lax.axis_index("tensor")
    z, y, c = lax.div(me, Y * CORES), lax.rem(lax.div(me, CORES), Y), lax.rem(me, CORES)
    g = z * CORES + c

    def group_member(i):
        h = lax.rem(g + G // 2 + (1 - 2 * lax.rem(i, 2)) * lax.div(i + 1, 2), G)
        return h, (lax.div(h, CORES) * Y + y) * CORES + lax.rem(h, CORES)

    def y_member(k):
        h = lax.rem(y + k, Y)
        return h, (z * Y + h) * CORES + c

    loads = [
        pltpu.make_async_copy(src, dst, load_sem.at[i])
        for i, (src, dst) in enumerate(
            ((down_hbm, down_vm), (up_hbm, up_vm), (cot_hbm, cot_vm), (weight_hbm, weight), (inputs_hbm, xs))
        )
    ]
    for load in loads:
        load.start()

    barrier = pltpu.get_barrier_semaphore()

    @pl.loop(0, G - 1)
    def _(i):
        _, device = group_member(i)
        pl.semaphore_signal(barrier, inc=1, device_id={"dp": device}, device_id_type=MESH)

    for k in (2, 1, 3):
        pl.semaphore_signal(barrier, inc=1, device_id={"dp": y_member(k)[1]}, device_id_type=MESH)
        pl.semaphore_signal(barrier, inc=1, device_id={"tensor": lax.rem(mx + k, X)}, device_id_type=MESH)

    lane0 = RANK * lax.rem(g, 8)
    block_of_lane = lax.div(lax.broadcasted_iota(jnp.int32, (RANK, LANES), 1), RANK)
    tenant = jnp.full((RANK, LANES), tenant_ref[0], jnp.int32).astype(F32)
    loads[0].wait()
    loads[1].wait()
    up = up_vm[0].astype(F32)
    for q in range(G):
        s1[q, :RANK, :] = down_vm[0, :, q * LANES : (q + 1) * LANES]
        tile = up[:, q // 8 * LANES : (q // 8 + 1) * LANES]
        s1[q, RANK:, :] = jnp.where(block_of_lane == q % 8, tile, tenant).astype(BF16)

    def group_exchange(step, src, dst):
        @pl.loop(0, G - 1)
        def _(i):
            h, device = group_member(i)
            pltpu.make_async_remote_copy(
                src.at[h], dst.at[g], send_sem.at[step], recv_sem.at[step],
                device_id={"dp": device}, device_id_type=MESH,
            ).start()

        pltpu.make_async_copy(src.at[g], dst.at[g], recv_sem.at[step]).start()

    def received(step, dst):
        pltpu.make_async_copy(dst, dst, recv_sem.at[step]).wait()

    pl.semaphore_wait(barrier, G - 1 + Y - 1 + X - 1)

    group_exchange(0, s1, r1)

    loads[2].wait()
    cot = cot_vm[...]
    loads[3].wait()
    shares = []
    for k in (2, 1, 3, 0):
        q = lax.rem(mx + k, X)

        @pl.loop(0, WIDTH // KEYS)
        def _(i):
            at = pl.multiple_of(q * WIDTH + i * KEYS, KEYS)
            product = dot(cot, weight[pl.ds(at, KEYS), :], ((1,), (1,)))
            columns = pl.ds(pl.multiple_of(i * KEYS, KEYS), KEYS)
            if k == 0:
                own[:, columns] = product
            else:
                partial[k - 1, :, columns] = product.astype(BF16)

        if k > 0:
            share = pltpu.make_async_remote_copy(
                partial.at[k - 1], arrived.at[k - 1], xsend_sem.at[k - 1], xrecv_sem.at[k - 1],
                device_id={"tensor": q}, device_id_type=MESH,
            )
            share.start()
            shares.append(share)

    key = lax.broadcasted_iota(jnp.int32, (KEYS, KEYS), 0)
    column = lax.broadcasted_iota(jnp.int32, (KEYS, KEYS), 1)
    target = lax.div(key, RANK) * LANES + lax.rem(key, RANK) + lane0
    for i in range(WIDTH // KEYS):
        spread = (column + i * KEYS == target).astype(F32).astype(BF16)
        cot_spread[:, i * KEYS : (i + 1) * KEYS] = dot(cot, spread).astype(BF16)
    loads[4].wait()
    received(0, r1)

    mine = r2.at[y]
    packed = [jnp.zeros((RANK, LANES), F32), jnp.zeros((RANK, LANES), F32)]
    tenants = []
    for h in range(G):
        mine[h * RANK : (h + 1) * RANK, :] = r1[h, :RANK, :]
        shift = lax.rem(RANK * (h % 8) + LANES - lane0, LANES)
        tile = pltpu.roll(r1[h, RANK:, :].astype(F32), shift, 1)
        packed[h // 8] = jnp.where(block_of_lane == h % 8, tile, packed[h // 8])
        tenants.append(tile)
    for q in range(2):
        mine[(G + q) * RANK : (G + q + 1) * RANK, :] = packed[q].astype(BF16)
    for k in (2, 1, 3):
        pltpu.make_async_remote_copy(
            mine, mine, send_sem.at[1], recv_sem.at[1],
            device_id={"dp": y_member(k)[1]}, device_id_type=MESH,
        ).start()

    rank_row = lax.broadcasted_iota(jnp.int32, (RANK, 1), 0)
    slot = lax.broadcasted_iota(jnp.int32, (RANK, Y * G * RANK), 1)
    for h in range(G):
        at = RANK * ((h + 1) % 8)
        t = tenants[h][:, at : at + 1].astype(jnp.int32)
        t_y, t_g = (t >> 1) & 3, (t >> 3) * 2 + (t & 1)
        wanted = (t_y * G + t_g) * RANK + rank_row
        pick[h * RANK : (h + 1) * RANK, :] = (slot == wanted).astype(F32).astype(BF16)

    def pick_of(q):
        return pick[:, q * KEYS : (q + 1) * KEYS]

    others = r2.at[pl.ds(0, Y - 1)]
    pltpu.make_async_copy(others, others, recv_sem.at[1]).wait()

    down_tiles = jnp.zeros((KEYS, LANES), F32)
    up_tiles = jnp.zeros((RANK, KEYS), F32)
    for q in range(Y):
        down_tiles += dot(pick_of(q), r2[q, : G * RANK, :])
        tiles = jnp.concatenate([r2[q, G * RANK : (G + 1) * RANK, :], r2[q, (G + 1) * RANK :, :]], axis=1)
        up_tiles += dot(tiles, pick_of(q), ((1,), (1,)))
    for h in range(G):
        s3[h, :RANK, :] = down_tiles[h * RANK : (h + 1) * RANK].astype(BF16)
        s3[h, RANK:, :] = up_tiles[:, h // 8 * LANES : (h // 8 + 1) * LANES].astype(BF16)
    group_exchange(2, s3, r3)
    received(2, r3)

    down_b = jnp.concatenate([r3[h, :RANK, :] for h in range(G)], axis=1)
    up_b = jnp.concatenate([r3[h, RANK:, :] for h in range(G)], axis=1)
    r4[mx, :RANK, :] = dot(down_b, xs[...], ((1,), (1,)))
    r4[mx, RANK:, :] = ADAPTER_SCALE * dot(up_b, cot_spread[...], ((1,), (1,)))
    for k in (2, 1, 3):
        pltpu.make_async_remote_copy(
            r4.at[mx], r4.at[mx], send_sem.at[3], recv_sem.at[3],
            device_id={"tensor": lax.rem(mx + k, X)}, device_id_type=MESH,
        ).start()
    others = r4.at[pl.ds(0, X - 1)]
    pltpu.make_async_copy(others, others, recv_sem.at[3]).wait()
    low = ((r4[0] + r4[1]) + (r4[2] + r4[3])).astype(BF16)
    low_in, low_out = low[:RANK], low[RANK:]

    for i in range(WIDTH // KEYS):
        columns = slice(i * KEYS, (i + 1) * KEYS)
        down_term = dot(low_out, xs[:, columns]).astype(BF16)
        up_term = (ADAPTER_SCALE * dot(low_in, cot_spread[:, columns])).astype(BF16)
        for q in range(2):
            s5[2 * i + q, :RANK, :] = down_term[:, q * LANES : (q + 1) * LANES]
            s5[2 * i + q, RANK:, :] = up_term[:, q * LANES : (q + 1) * LANES]
    group_exchange(4, s5, r5)
    for i in range(WIDTH // KEYS):
        columns = slice(i * KEYS, (i + 1) * KEYS)
        own[:, columns] += dot(low_out, down_b[:, columns], ((0,), (0,)))
    received(4, r5)

    down_terms = r5[:, :RANK, :].reshape(G * RANK, LANES)
    packed = []
    for q in range(2):
        total = r5[8 * q, RANK:, :].astype(F32)
        for h in range(8 * q + 1, 8 * q + 8):
            total += r5[h, RANK:, :].astype(F32)
        packed.append(total.astype(BF16))
    up_terms = jnp.concatenate(packed, axis=1)
    for q in range(Y):
        s6[q, : G * RANK, :] = dot(pick_of(q), down_terms, ((0,), (0,))).astype(BF16)
        sums = dot(up_terms, pick_of(q)).astype(BF16)
        s6[q, G * RANK : (G + 1) * RANK, :] = sums[:, :LANES]
        s6[q, (G + 1) * RANK :, :] = sums[:, LANES:]
    for k in (2, 1, 3):
        h, device = y_member(k)
        pltpu.make_async_remote_copy(
            s6.at[h], r6.at[y], send_sem.at[5], recv_sem.at[5],
            device_id={"dp": device}, device_id_type=MESH,
        ).start()
    pltpu.make_async_copy(s6.at[y], r6.at[y], recv_sem.at[5]).start()
    received(5, r6)

    for h in range(G + 2):
        rows = slice(h * RANK, (h + 1) * RANK)
        total = (r6[0, rows, :].astype(F32) + r6[1, rows, :].astype(F32)) + (
            r6[2, rows, :].astype(F32) + r6[3, rows, :].astype(F32)
        )
        if h < G:
            s7[h, :RANK, :] = total
        else:
            for owner in range(8 * (h - G), 8 * (h - G) + 8):
                s7[owner, RANK:, :] = total
    group_exchange(6, s7, r7)

    for share in shares:
        share.wait()
    for i in range(WIDTH // KEYS):
        columns = slice(i * KEYS, (i + 1) * KEYS)
        total = own[:, columns]
        for k in range(X - 1):
            total += arrived[k, :, columns].astype(F32)
        out_vm[:, columns] = total.astype(BF16)
    stores = [
        pltpu.make_async_copy(src, dst, store_sem.at[i])
        for i, (src, dst) in enumerate(((out_vm, out_hbm), (grad_down, grad_down_hbm), (grad_up, grad_up_hbm)))
    ]
    stores[0].start()
    received(6, r7)

    for h in range(G):
        grad_down[0, :, h * LANES : (h + 1) * LANES] = r7[h, :RANK, :]
    stores[1].start()
    for q in range(2):
        total = jnp.zeros((RANK, LANES), F32)
        for h in range(8 * q, 8 * q + 8):
            moved = pltpu.roll(r7[h, RANK:, :], lax.rem(RANK * (h % 8) + LANES - lane0, LANES), 1)
            total = jnp.where(block_of_lane == h % 8, moved, total)
        grad_up[0, :, q * LANES : (q + 1) * LANES] = total

    stores[2].start()

    for store in stores:
        store.wait()
    for step, sent in ((0, s1), (2, s3), (4, s5), (6, s7)):
        peers = sent.at[pl.ds(0, G - 1)]
        pltpu.make_async_copy(peers, peers, send_sem.at[step]).wait()
    for step, sent in ((1, r2), (3, r4), (5, s6)):
        peers = sent.at[pl.ds(0, 3)]
        pltpu.make_async_copy(peers, peers, send_sem.at[step]).wait()


def on_device(inputs, cotangent, frozen_key_weight, adapter_down_weight, adapter_up_weight, tenant_per_block):
    hbm = pl.BlockSpec(memory_space=pl.ANY)
    smem = pl.BlockSpec(memory_space=pltpu.SMEM)
    dma = pltpu.SemaphoreType.DMA
    return pl.pallas_call(
        kernel,
        out_shape=(
            jax.ShapeDtypeStruct((ROWS, WIDTH), BF16),
            jax.ShapeDtypeStruct((1, RANK, WIDTH), F32),
            jax.ShapeDtypeStruct((1, RANK, KEYS), F32),
        ),
        in_specs=[hbm] * 5 + [smem],
        out_specs=(hbm, hbm, hbm),
        scratch_shapes=[
            pltpu.VMEM((ROWS, WIDTH), BF16),
            pltpu.VMEM((ROWS, KEYS), BF16),
            pltpu.VMEM((X * WIDTH, KEYS), BF16),
            pltpu.VMEM((1, RANK, WIDTH), BF16),
            pltpu.VMEM((1, RANK, KEYS), BF16),
            pltpu.VMEM((X - 1, ROWS, WIDTH), BF16),
            pltpu.VMEM((ROWS, WIDTH), F32),
            pltpu.VMEM((X - 1, ROWS, WIDTH), BF16),
            pltpu.VMEM((ROWS, WIDTH), BF16),
            pltpu.VMEM((1, RANK, WIDTH), F32),
            pltpu.VMEM((1, RANK, KEYS), F32),
            pltpu.VMEM((ROWS, WIDTH), BF16),
            pltpu.VMEM((G * RANK, Y * G * RANK), BF16),
            pltpu.VMEM((G, 2 * RANK, LANES), BF16),
            pltpu.VMEM((G, 2 * RANK, LANES), BF16),
            pltpu.VMEM((Y, TABLE, LANES), BF16),
            pltpu.VMEM((G, 2 * RANK, LANES), BF16),
            pltpu.VMEM((G, 2 * RANK, LANES), BF16),
            pltpu.VMEM((X, 2 * RANK, LANES), F32),
            pltpu.VMEM((G, 2 * RANK, LANES), BF16),
            pltpu.VMEM((G, 2 * RANK, LANES), BF16),
            pltpu.VMEM((Y, TABLE, LANES), BF16),
            pltpu.VMEM((Y, TABLE, LANES), BF16),
            pltpu.VMEM((G, 2 * RANK, LANES), F32),
            pltpu.VMEM((G, 2 * RANK, LANES), F32),
            dma((5,)), dma((3,)), dma((7,)), dma((7,)), dma((X - 1,)), dma((X - 1,)),
        ],
        compiler_params=pltpu.CompilerParams(
            collective_id=0, has_side_effects=True, vmem_limit_bytes=60 << 20
        ),
    )(inputs, cotangent, frozen_key_weight, adapter_down_weight, adapter_up_weight, tenant_per_block)


def solution(mesh):
    in_specs = (
        P("dp", "tensor"),
        P("dp", "tensor"),
        P(None, "tensor"),
        P("dp", None, "tensor"),
        P("dp", None, "tensor"),
        P("dp"),
    )
    out_specs = (P("dp", "tensor"), P("dp", None, "tensor"), P("dp", None, "tensor"))
    return jax.shard_map(
        on_device, mesh=mesh, in_specs=in_specs, out_specs=out_specs, check_vma=False
    )
```

```python
import jax
import jax.numpy as jnp
from jax import lax
from jax.experimental import pallas as pl
from jax.experimental.pallas import tpu as pltpu
from jax.sharding import PartitionSpec as P

MESH = pl.DeviceIdType.MESH
F32 = jnp.float32
BF16 = jnp.bfloat16
ADAPTER_SCALE = 2.0

Z, Y, CORES, X = 8, 4, 2, 4
G = Z * CORES
ROWS, WIDTH, KEYS, RANK, LANES = 128, 2048, 256, 16, 128
TABLE = G * RANK + 2 * RANK


def dot(a, b, dims=((1,), (0,))):
    return lax.dot_general(a, b, (dims, ((), ())), preferred_element_type=F32)


def kernel(
    inputs_hbm, cot_hbm, weight_hbm, down_hbm, up_hbm, tenant_ref,
    out_hbm, grad_down_hbm, grad_up_hbm,
    xs, cot_vm, weight, down_vm, up_vm, partial, own, arrived, out_vm, grad_down, grad_up, cot_spread, pick,
    s1, r1, r2, s3, r3, r4, s5, r5, s6, r6, s7, r7, s7u, r7u,
    load_sem, store_sem, send_sem, recv_sem, xsend_sem, xrecv_sem,
):
    me, mx = lax.axis_index("dp"), lax.axis_index("tensor")
    z, y, c = lax.div(me, Y * CORES), lax.rem(lax.div(me, CORES), Y), lax.rem(me, CORES)
    g = z * CORES + c

    def group_member(i):
        h = lax.rem(g + G // 2 + (1 - 2 * lax.rem(i, 2)) * lax.div(i + 1, 2), G)
        return h, (lax.div(h, CORES) * Y + y) * CORES + lax.rem(h, CORES)

    def y_member(k):
        h = lax.rem(y + k, Y)
        return h, (z * Y + h) * CORES + c

    loads = [
        pltpu.make_async_copy(src, dst, load_sem.at[i])
        for i, (src, dst) in enumerate(
            ((down_hbm, down_vm), (up_hbm, up_vm), (cot_hbm, cot_vm), (weight_hbm, weight), (inputs_hbm, xs))
        )
    ]
    for load in loads:
        load.start()

    barrier = pltpu.get_barrier_semaphore()

    @pl.loop(0, G - 1)
    def _(i):
        _, device = group_member(i)
        pl.semaphore_signal(barrier, inc=1, device_id={"dp": device}, device_id_type=MESH)

    for k in (2, 1, 3):
        pl.semaphore_signal(barrier, inc=1, device_id={"dp": y_member(k)[1]}, device_id_type=MESH)
        pl.semaphore_signal(barrier, inc=1, device_id={"tensor": lax.rem(mx + k, X)}, device_id_type=MESH)

    lane0 = RANK * lax.rem(g, 8)
    block_of_lane = lax.div(lax.broadcasted_iota(jnp.int32, (RANK, LANES), 1), RANK)
    tenant = jnp.full((RANK, LANES), tenant_ref[0], jnp.int32).astype(F32)
    loads[0].wait()
    loads[1].wait()
    up = up_vm[0].astype(F32)
    for q in range(G):
        s1[q, :RANK, :] = down_vm[0, :, q * LANES : (q + 1) * LANES]
        tile = up[:, q // 8 * LANES : (q // 8 + 1) * LANES]
        s1[q, RANK:, :] = jnp.where(block_of_lane == q % 8, tile, tenant).astype(BF16)

    def group_exchange(step, src, dst):
        @pl.loop(0, G - 1)
        def _(i):
            h, device = group_member(i)
            pltpu.make_async_remote_copy(
                src.at[h], dst.at[g], send_sem.at[step], recv_sem.at[step],
                device_id={"dp": device}, device_id_type=MESH,
            ).start()

        pltpu.make_async_copy(src.at[g], dst.at[g], recv_sem.at[step]).start()

    def received(step, dst):
        pltpu.make_async_copy(dst, dst, recv_sem.at[step]).wait()

    pl.semaphore_wait(barrier, G - 1 + Y - 1 + X - 1)

    group_exchange(0, s1, r1)

    loads[2].wait()
    cot = cot_vm[...]
    loads[3].wait()
    shares = []
    for k in (1, 3, 2, 0):
        q = lax.rem(mx + k, X)
        product = dot(cot, weight[pl.ds(pl.multiple_of(q * WIDTH, WIDTH), WIDTH), :], ((1,), (1,)))
        if k == 0:
            own[...] = product
        else:
            partial[k - 1] = product.astype(BF16)
            shares.append(
                pltpu.make_async_remote_copy(
                    partial.at[k - 1], arrived.at[k - 1], xsend_sem.at[k - 1], xrecv_sem.at[k - 1],
                    device_id={"tensor": q}, device_id_type=MESH,
                )
            )
            if k != 2:
                shares[-1].start()

    key = lax.broadcasted_iota(jnp.int32, (KEYS, KEYS), 0)
    column = lax.broadcasted_iota(jnp.int32, (KEYS, KEYS), 1)
    target = lax.div(key, RANK) * LANES + lax.rem(key, RANK) + lane0
    for i in range(WIDTH // KEYS):
        spread = (column + i * KEYS == target).astype(F32).astype(BF16)
        cot_spread[:, i * KEYS : (i + 1) * KEYS] = dot(cot, spread).astype(BF16)
    loads[4].wait()
    received(0, r1)

    mine = r2.at[y]
    packed = [jnp.zeros((RANK, LANES), F32), jnp.zeros((RANK, LANES), F32)]
    tenants = []
    for h in range(G):
        mine[h * RANK : (h + 1) * RANK, :] = r1[h, :RANK, :]
        shift = lax.rem(RANK * (h % 8) + LANES - lane0, LANES)
        tile = pltpu.roll(r1[h, RANK:, :].astype(F32), shift, 1)
        packed[h // 8] = jnp.where(block_of_lane == h % 8, tile, packed[h // 8])
        tenants.append(tile)
    for q in range(2):
        mine[(G + q) * RANK : (G + q + 1) * RANK, :] = packed[q].astype(BF16)
    for k in (2, 1, 3):
        pltpu.make_async_remote_copy(
            mine, mine, send_sem.at[1], recv_sem.at[1],
            device_id={"dp": y_member(k)[1]}, device_id_type=MESH,
        ).start()

    rank_row = lax.broadcasted_iota(jnp.int32, (RANK, 1), 0)
    slot = lax.broadcasted_iota(jnp.int32, (RANK, Y * G * RANK), 1)
    for h in range(G):
        at = RANK * ((h + 1) % 8)
        t = tenants[h][:, at : at + 1].astype(jnp.int32)
        t_y, t_g = (t >> 1) & 3, (t >> 3) * 2 + (t & 1)
        wanted = (t_y * G + t_g) * RANK + rank_row
        pick[h * RANK : (h + 1) * RANK, :] = (slot == wanted).astype(F32).astype(BF16)

    def pick_of(q):
        return pick[:, q * KEYS : (q + 1) * KEYS]

    others = r2.at[pl.ds(0, Y - 1)]
    pltpu.make_async_copy(others, others, recv_sem.at[1]).wait()

    down_tiles = jnp.zeros((KEYS, LANES), F32)
    up_tiles = jnp.zeros((RANK, KEYS), F32)
    for q in range(Y):
        down_tiles += dot(pick_of(q), r2[q, : G * RANK, :])
        tiles = jnp.concatenate([r2[q, G * RANK : (G + 1) * RANK, :], r2[q, (G + 1) * RANK :, :]], axis=1)
        up_tiles += dot(tiles, pick_of(q), ((1,), (1,)))
    for h in range(G):
        s3[h, :RANK, :] = down_tiles[h * RANK : (h + 1) * RANK].astype(BF16)
        s3[h, RANK:, :] = up_tiles[:, h // 8 * LANES : (h // 8 + 1) * LANES].astype(BF16)
    group_exchange(2, s3, r3)
    received(2, r3)

    down_b = jnp.concatenate([r3[h, :RANK, :] for h in range(G)], axis=1)
    up_b = jnp.concatenate([r3[h, RANK:, :] for h in range(G)], axis=1)
    r4[mx, :RANK, :] = dot(down_b, xs[...], ((1,), (1,)))
    r4[mx, RANK:, :] = ADAPTER_SCALE * dot(up_b, cot_spread[...], ((1,), (1,)))
    for k in (2, 1, 3):
        pltpu.make_async_remote_copy(
            r4.at[mx], r4.at[mx], send_sem.at[3], recv_sem.at[3],
            device_id={"tensor": lax.rem(mx + k, X)}, device_id_type=MESH,
        ).start()
    shares[2].start()
    others = r4.at[pl.ds(0, X - 1)]
    pltpu.make_async_copy(others, others, recv_sem.at[3]).wait()
    low = ((r4[0] + r4[1]) + (r4[2] + r4[3])).astype(BF16)
    low_in, low_out = low[:RANK], low[RANK:]

    for i in range(WIDTH // KEYS):
        columns = slice(i * KEYS, (i + 1) * KEYS)
        down_term = dot(low_out, xs[:, columns]).astype(BF16)
        up_term = (ADAPTER_SCALE * dot(low_in, cot_spread[:, columns])).astype(BF16)
        for q in range(2):
            s5[2 * i + q, :RANK, :] = down_term[:, q * LANES : (q + 1) * LANES]
            s5[2 * i + q, RANK:, :] = up_term[:, q * LANES : (q + 1) * LANES]
    group_exchange(4, s5, r5)
    for i in range(WIDTH // KEYS):
        columns = slice(i * KEYS, (i + 1) * KEYS)
        own[:, columns] += dot(low_out, down_b[:, columns], ((0,), (0,)))
    received(4, r5)

    down_terms = r5[:, :RANK, :].reshape(G * RANK, LANES)
    packed = []
    for q in range(2):
        total = r5[8 * q, RANK:, :].astype(F32)
        for h in range(8 * q + 1, 8 * q + 8):
            total += r5[h, RANK:, :].astype(F32)
        packed.append(total.astype(BF16))
    up_terms = jnp.concatenate(packed, axis=1)
    for q in range(Y):
        s6[q, : G * RANK, :] = dot(pick_of(q), down_terms, ((0,), (0,))).astype(BF16)
        sums = dot(up_terms, pick_of(q)).astype(BF16)
        s6[q, G * RANK : (G + 1) * RANK, :] = sums[:, :LANES]
        s6[q, (G + 1) * RANK :, :] = sums[:, LANES:]
    for k in (2, 1, 3):
        h, device = y_member(k)
        pltpu.make_async_remote_copy(
            s6.at[h], r6.at[y], send_sem.at[5], recv_sem.at[5],
            device_id={"dp": device}, device_id_type=MESH,
        ).start()
    pltpu.make_async_copy(s6.at[y], r6.at[y], recv_sem.at[5]).start()
    received(5, r6)

    half = RANK // 2
    row = lax.broadcasted_iota(jnp.int32, (half, LANES), 0)
    block = lax.div(lax.broadcasted_iota(jnp.int32, (half, LANES), 1), RANK)
    for h in range(G + 2):
        rows = slice(h * RANK, (h + 1) * RANK)
        total = (r6[0, rows, :].astype(F32) + r6[1, rows, :].astype(F32)) + (
            r6[2, rows, :].astype(F32) + r6[3, rows, :].astype(F32)
        )
        if h < G:
            s7[h] = total
            continue
        for i in range(2):
            ranks = total[half * i : half * (i + 1)]
            turned = ranks
            for j in range(1, half):
                turned = jnp.where(row == j, pltpu.roll(ranks, j * RANK, 1), turned)
            for j in range(half):
                chosen = jnp.where(block == lax.rem(row + j, half), turned, 0.0)
                s7u[half * (h - G) + j, i : i + 1, :] = jnp.sum(chosen, axis=0, keepdims=True)
    group_exchange(6, s7, r7)
    group_exchange(7, s7u, r7u)

    for share in shares:
        share.wait()
    for i in range(WIDTH // KEYS):
        columns = slice(i * KEYS, (i + 1) * KEYS)
        total = own[:, columns]
        for k in range(X - 1):
            total += arrived[k, :, columns].astype(F32)
        out_vm[:, columns] = total.astype(BF16)
    stores = [
        pltpu.make_async_copy(src, dst, store_sem.at[i])
        for i, (src, dst) in enumerate(((out_vm, out_hbm), (grad_down, grad_down_hbm), (grad_up, grad_up_hbm)))
    ]
    stores[0].start()
    received(6, r7)

    for h in range(G):
        grad_down[0, :, h * LANES : (h + 1) * LANES] = r7[h, :RANK, :]
    stores[1].start()
    received(7, r7u)
    mine = block == lax.rem(row + lax.rem(g, half), half)
    for q in range(2):
        for i in range(2):
            turned = jnp.zeros((half, LANES), F32)
            for h in range(half):
                value = jnp.broadcast_to(r7u[half * q + h, i : i + 1, :], (half, LANES))
                turned += pltpu.roll(jnp.where(mine, value, 0.0), h * RANK, 1)
            turned = pltpu.roll(turned, lax.rem(LANES - lane0, LANES), 1)
            total = turned
            for j in range(1, half):
                total = jnp.where(row == j, pltpu.roll(turned, LANES - j * RANK, 1), total)
            grad_up[0, half * i : half * (i + 1), q * LANES : (q + 1) * LANES] = total
    stores[2].start()

    for store in stores:
        store.wait()
    for step, sent in ((0, s1), (2, s3), (4, s5), (6, s7), (7, s7u)):
        peers = sent.at[pl.ds(0, G - 1)]
        pltpu.make_async_copy(peers, peers, send_sem.at[step]).wait()
    for step, sent in ((1, r2), (3, r4), (5, s6)):
        peers = sent.at[pl.ds(0, 3)]
        pltpu.make_async_copy(peers, peers, send_sem.at[step]).wait()


def on_device(inputs, cotangent, frozen_key_weight, adapter_down_weight, adapter_up_weight, tenant_per_block):
    hbm = pl.BlockSpec(memory_space=pl.ANY)
    smem = pl.BlockSpec(memory_space=pltpu.SMEM)
    dma = pltpu.SemaphoreType.DMA
    return pl.pallas_call(
        kernel,
        out_shape=(
            jax.ShapeDtypeStruct((ROWS, WIDTH), BF16),
            jax.ShapeDtypeStruct((1, RANK, WIDTH), F32),
            jax.ShapeDtypeStruct((1, RANK, KEYS), F32),
        ),
        in_specs=[hbm] * 5 + [smem],
        out_specs=(hbm, hbm, hbm),
        scratch_shapes=[
            pltpu.VMEM((ROWS, WIDTH), BF16),
            pltpu.VMEM((ROWS, KEYS), BF16),
            pltpu.VMEM((X * WIDTH, KEYS), BF16),
            pltpu.VMEM((1, RANK, WIDTH), BF16),
            pltpu.VMEM((1, RANK, KEYS), BF16),
            pltpu.VMEM((X - 1, ROWS, WIDTH), BF16),
            pltpu.VMEM((ROWS, WIDTH), F32),
            pltpu.VMEM((X - 1, ROWS, WIDTH), BF16),
            pltpu.VMEM((ROWS, WIDTH), BF16),
            pltpu.VMEM((1, RANK, WIDTH), F32),
            pltpu.VMEM((1, RANK, KEYS), F32),
            pltpu.VMEM((ROWS, WIDTH), BF16),
            pltpu.VMEM((G * RANK, Y * G * RANK), BF16),
            pltpu.VMEM((G, 2 * RANK, LANES), BF16),
            pltpu.VMEM((G, 2 * RANK, LANES), BF16),
            pltpu.VMEM((Y, TABLE, LANES), BF16),
            pltpu.VMEM((G, 2 * RANK, LANES), BF16),
            pltpu.VMEM((G, 2 * RANK, LANES), BF16),
            pltpu.VMEM((X, 2 * RANK, LANES), F32),
            pltpu.VMEM((G, 2 * RANK, LANES), BF16),
            pltpu.VMEM((G, 2 * RANK, LANES), BF16),
            pltpu.VMEM((Y, TABLE, LANES), BF16),
            pltpu.VMEM((Y, TABLE, LANES), BF16),
            pltpu.VMEM((G, RANK, LANES), F32),
            pltpu.VMEM((G, RANK, LANES), F32),
            pltpu.VMEM((G, 2, LANES), F32),
            pltpu.VMEM((G, 2, LANES), F32),
            dma((5,)), dma((3,)), dma((8,)), dma((8,)), dma((X - 1,)), dma((X - 1,)),
        ],
        compiler_params=pltpu.CompilerParams(
            collective_id=0, has_side_effects=True, vmem_limit_bytes=60 << 20
        ),
    )(inputs, cotangent, frozen_key_weight, adapter_down_weight, adapter_up_weight, tenant_per_block)


def solution(mesh):
    in_specs = (
        P("dp", "tensor"),
        P("dp", "tensor"),
        P(None, "tensor"),
        P("dp", None, "tensor"),
        P("dp", None, "tensor"),
        P("dp"),
    )
    out_specs = (P("dp", "tensor"), P("dp", None, "tensor"), P("dp", None, "tensor"))
    return jax.shard_map(
        on_device, mesh=mesh, in_specs=in_specs, out_specs=out_specs, check_vma=False
    )
```

```python
import jax
import jax.numpy as jnp
from jax import lax
from jax.experimental import pallas as pl
from jax.experimental.pallas import tpu as pltpu
from jax.sharding import PartitionSpec as P

MESH = pl.DeviceIdType.MESH
F32 = jnp.float32
BF16 = jnp.bfloat16
ADAPTER_SCALE = 2.0

Z, Y, CORES, X = 8, 4, 2, 4
G = Z * CORES
ROWS, WIDTH, KEYS, RANK, LANES = 128, 2048, 256, 16, 128
HALF, SPLIT = 64, 80

STEPS = 14
UP_ALL, ID_Y, DOWN_IN, ID_G, UP_PICK, DOWN_ALL, OUT_SUM, DOWN_PICK, TERM, IN_SUM, TERM_Y, UP_TERM, TERM_OWNER, UP_TERM_Y = range(STEPS)


def dot(a, b, dims=((1,), (0,))):
    return lax.dot_general(a, b, (dims, ((), ())), preferred_element_type=F32)


def kernel(
    inputs_hbm, cot_hbm, weight_hbm, down_hbm, up_hbm, tenant_ref,
    out_ref, grad_down_ref, grad_up_ref,
    xs, cot_vm, weight, down_vm, up_vm, partial, own, arrived, hop, ids, pick,
    up_all, id_y, down_in, down_all, id_g, up_send, up_recv, out_sum, down_send, down_recv, in_sum,
    term_send, term_recv, term_y_send, term_y_recv, term_owner_send, term_owner_recv,
    up_term, up_term_all, up_term_y_send, up_term_y_recv,
    load_sem, send_sem, recv_sem, xsend_sem, xrecv_sem,
):
    me, mx = lax.axis_index("dp"), lax.axis_index("tensor")
    z, y, c = lax.div(me, Y * CORES), lax.rem(lax.div(me, CORES), Y), lax.rem(me, CORES)
    g = z * CORES + c
    x_next, x_last = lax.rem(mx + 1, X), lax.rem(mx + X - 1, X)

    def group_member(i):
        h = lax.rem(g + G // 2 + (1 - 2 * lax.rem(i, 2)) * lax.div(i + 1, 2), G)
        return h, (lax.div(h, CORES) * Y + y) * CORES + lax.rem(h, CORES)

    def y_member(k):
        h = lax.rem(y + k, Y)
        return h, (z * Y + h) * CORES + c

    def send(step, src, dst, axis, device):
        pltpu.make_async_remote_copy(
            src, dst, send_sem.at[step], recv_sem.at[step], device_id={axis: device}, device_id_type=MESH
        ).start()

    def keep(step, src, dst):
        pltpu.make_async_copy(src, dst, recv_sem.at[step]).start()

    def received(step, dst):
        pltpu.make_async_copy(dst, dst, recv_sem.at[step]).wait()

    loads = [
        pltpu.make_async_copy(src, dst, load_sem.at[i])
        for i, (src, dst) in enumerate(
            ((up_hbm, up_vm), (down_hbm, down_vm), (cot_hbm, cot_vm), (weight_hbm, weight), (inputs_hbm, xs))
        )
    ]
    for load in loads:
        load.start()

    barrier = pltpu.get_barrier_semaphore()

    @pl.loop(0, G - 1)
    def _(i):
        _, device = group_member(i)
        pl.semaphore_signal(barrier, inc=1, device_id={"dp": device}, device_id_type=MESH)

    for k in (2, 1, 3):
        pl.semaphore_signal(barrier, inc=1, device_id={"dp": y_member(k)[1]}, device_id_type=MESH)
        pl.semaphore_signal(barrier, inc=1, device_id={"tensor": lax.rem(mx + k, X)}, device_id_type=MESH)

    ids[0] = jnp.full((1, LANES), tenant_ref[0], jnp.int32).astype(F32)
    loads[0].wait()
    loads[1].wait()
    for q in range(G):
        down_in[q] = down_vm[0, :, q * LANES : (q + 1) * LANES]
    pl.semaphore_wait(barrier, G - 1 + Y - 1 + X - 1)

    @pl.loop(0, G - 1)
    def _(i):
        send(UP_ALL, up_vm.at[0], up_all.at[g], "dp", group_member(i)[1])

    keep(UP_ALL, up_vm.at[0], up_all.at[g])
    for k in (2, 1, 3):
        send(ID_Y, ids.at[0], id_y.at[y], "dp", y_member(k)[1])
    keep(ID_Y, ids.at[0], id_y.at[y])
    my_rows = pl.ds(pl.multiple_of(g * RANK, RANK), RANK)

    @pl.loop(0, G - 1)
    def _(i):
        h, device = group_member(i)
        send(DOWN_IN, down_in.at[h], down_all.at[y, my_rows], "dp", device)

    keep(DOWN_IN, down_in.at[g], down_all.at[y, my_rows])

    @pl.loop(0, G - 1)
    def _(i):
        send(ID_G, ids.at[0], id_g.at[g], "dp", group_member(i)[1])

    keep(ID_G, ids.at[0], id_g.at[g])

    def share(i, src, dst, device):
        return pltpu.make_async_remote_copy(
            src, dst, xsend_sem.at[i], xrecv_sem.at[i], device_id={"tensor": device}, device_id_type=MESH
        )

    low_half, high_half = pl.ds(0, HALF), pl.ds(HALF, ROWS - HALF)
    first, rest = pl.ds(0, SPLIT), pl.ds(SPLIT, ROWS - SPLIT)
    hops = (
        share(0, partial.at[1, low_half], hop.at[0], x_next),
        share(1, partial.at[1, high_half], hop.at[1], x_last),
    )
    nearby = (
        share(2, partial.at[0, first], arrived.at[0, first], x_next),
        share(3, partial.at[2, first], arrived.at[2, first], x_last),
    )
    last = (
        share(4, partial.at[0, rest], arrived.at[0, rest], x_next),
        share(5, partial.at[2, rest], arrived.at[2, rest], x_last),
        share(6, hop.at[0], arrived.at[1, low_half], x_next),
        share(7, hop.at[1], arrived.at[1, high_half], x_last),
    )
    loads[2].wait()
    cot = cot_vm[...]
    loads[3].wait()
    for k in (2, 1, 3, 0):
        at = pl.multiple_of(lax.rem(mx + k, X) * WIDTH, WIDTH)
        product = dot(cot, weight[pl.ds(at, WIDTH), :], ((1,), (1,)))
        if k == 0:
            own[...] = product
        else:
            partial[k - 1] = product.astype(BF16)
        if k == 2:
            for copy in hops:
                copy.start()

    def place(t):
        t = t.astype(jnp.int32)
        return (t >> 1) & 3, (t >> 3) * CORES + (t & 1)

    rank = lax.broadcasted_iota(jnp.int32, (RANK, 1), 0)
    slot = lax.broadcasted_iota(jnp.int32, (RANK, G * RANK), 1)
    received(ID_Y, id_y)
    wanted = []
    for h in range(Y):
        t_y, t_g = place(jnp.broadcast_to(id_y[h, :, :1], (RANK, 1)))
        wanted.append((slot == jnp.where(t_y == y, t_g * RANK + rank, -1)).astype(F32).astype(BF16))
    wanted = jnp.concatenate(wanted, axis=0)
    received(UP_ALL, up_all)
    chosen = dot(wanted, up_all[...].reshape(G * RANK, KEYS)).astype(BF16)
    for h in range(Y):
        up_send[h] = chosen[h * RANK : (h + 1) * RANK]
    for k in (2, 1, 3):
        h, device = y_member(k)
        send(UP_PICK, up_send.at[h], up_recv.at[y], "dp", device)
    keep(UP_PICK, up_send.at[y], up_recv.at[y])

    received(DOWN_IN, down_all.at[y])
    for k in (2, 1, 3):
        send(DOWN_ALL, down_all.at[y], down_all.at[y], "dp", y_member(k)[1])

    received(ID_G, id_g)
    slot = lax.broadcasted_iota(jnp.int32, (RANK, Y * G * RANK), 1)
    column = lax.broadcasted_iota(jnp.int32, (RANK, Y * RANK), 1)
    mine = []
    for h in range(G):
        t_y, t_g = place(jnp.broadcast_to(id_g[h, :, :1], (RANK, 1)))
        pick[h * RANK : (h + 1) * RANK, :] = (slot == (t_y * G + t_g) * RANK + rank).astype(F32).astype(BF16)
        mine.append((column == jnp.where(t_g == g, t_y * RANK + rank, -1)).astype(F32).astype(BF16))
    mine = jnp.concatenate(mine, axis=0)

    def pick_of(q):
        return pick[:, q * G * RANK : (q + 1) * G * RANK]

    received(UP_PICK, up_recv)
    up_b = (up_recv[0].astype(F32) + up_recv[1].astype(F32)) + (up_recv[2].astype(F32) + up_recv[3].astype(F32))
    out_sum[mx] = ADAPTER_SCALE * dot(up_b.astype(BF16), cot, ((1,), (1,)))
    for k in (2, 1, 3):
        send(OUT_SUM, out_sum.at[mx], out_sum.at[mx], "tensor", lax.rem(mx + k, X))
    for copy in nearby:
        copy.start()

    received(DOWN_ALL, down_all.at[pl.ds(0, Y - 1)])
    tiles = jnp.zeros((G * RANK, LANES), F32)
    for q in range(Y):
        tiles += dot(pick_of(q), down_all[q])
    for h in range(G):
        down_send[h] = tiles[h * RANK : (h + 1) * RANK].astype(BF16)

    @pl.loop(0, G - 1)
    def _(i):
        h, device = group_member(i)
        send(DOWN_PICK, down_send.at[h], down_recv.at[g], "dp", device)

    keep(DOWN_PICK, down_send.at[g], down_recv.at[g])

    loads[4].wait()
    received(OUT_SUM, out_sum.at[pl.ds(0, X - 1)])
    low_out = ((out_sum[0] + out_sum[1]) + (out_sum[2] + out_sum[3])).astype(BF16)
    term = dot(low_out, xs[...]).astype(BF16)
    for h in range(G):
        term_send[h] = term[:, h * LANES : (h + 1) * LANES]

    @pl.loop(0, G - 1)
    def _(i):
        h, device = group_member(i)
        send(TERM, term_send.at[h], term_recv.at[g], "dp", device)

    keep(TERM, term_send.at[g], term_recv.at[g])

    received(DOWN_PICK, down_recv)
    down_b = jnp.concatenate([down_recv[h] for h in range(G)], axis=1)
    in_sum[mx] = dot(down_b, xs[...], ((1,), (1,)))
    for k in (2, 1, 3):
        send(IN_SUM, in_sum.at[mx], in_sum.at[mx], "tensor", lax.rem(mx + k, X))
    for copy in hops:
        copy.wait_recv()
    for copy in last:
        copy.start()
    own[...] += dot(low_out, down_b, ((0,), (0,)))

    received(TERM, term_recv)
    terms = term_recv[...].reshape(G * RANK, LANES)
    for q in range(Y):
        term_y_send[q] = dot(pick_of(q), terms, ((0,), (0,))).astype(BF16)
    for k in (2, 1, 3):
        h, device = y_member(k)
        send(TERM_Y, term_y_send.at[h], term_y_recv.at[y], "dp", device)
    keep(TERM_Y, term_y_send.at[y], term_y_recv.at[y])

    received(IN_SUM, in_sum.at[pl.ds(0, X - 1)])
    low_in = ((in_sum[0] + in_sum[1]) + (in_sum[2] + in_sum[3])).astype(BF16)
    up_term[...] = (ADAPTER_SCALE * dot(low_in, cot)).astype(BF16)

    @pl.loop(0, G - 1)
    def _(i):
        send(UP_TERM, up_term, up_term_all.at[g], "dp", group_member(i)[1])

    keep(UP_TERM, up_term, up_term_all.at[g])

    received(TERM_Y, term_y_recv)
    for h in range(G):
        rows = slice(h * RANK, (h + 1) * RANK)
        term_owner_send[h] = (term_y_recv[0, rows].astype(F32) + term_y_recv[1, rows].astype(F32)) + (
            term_y_recv[2, rows].astype(F32) + term_y_recv[3, rows].astype(F32)
        )

    @pl.loop(0, G - 1)
    def _(i):
        h, device = group_member(i)
        send(TERM_OWNER, term_owner_send.at[h], term_owner_recv.at[g], "dp", device)

    keep(TERM_OWNER, term_owner_send.at[g], term_owner_recv.at[g])

    received(UP_TERM, up_term_all)
    sums = dot(mine, up_term_all[...].reshape(G * RANK, KEYS), ((0,), (0,)))
    for h in range(Y):
        up_term_y_send[h] = sums[h * RANK : (h + 1) * RANK]
    for k in (2, 1, 3):
        h, device = y_member(k)
        send(UP_TERM_Y, up_term_y_send.at[h], up_term_y_recv.at[y], "dp", device)
    keep(UP_TERM_Y, up_term_y_send.at[y], up_term_y_recv.at[y])

    for copy in nearby + last:
        copy.wait_recv()
    for i in range(WIDTH // KEYS):
        columns = slice(i * KEYS, (i + 1) * KEYS)
        total = own[:, columns]
        for k in range(X - 1):
            total += arrived[k, :, columns].astype(F32)
        out_ref[:, columns] = total.astype(BF16)
    received(TERM_OWNER, term_owner_recv)
    for h in range(G):
        grad_down_ref[0, :, h * LANES : (h + 1) * LANES] = term_owner_recv[h]
    received(UP_TERM_Y, up_term_y_recv)
    grad_up_ref[0] = (up_term_y_recv[0] + up_term_y_recv[1]) + (up_term_y_recv[2] + up_term_y_recv[3])

    for copy in hops + nearby + last:
        copy.wait_send()
    for step, sent, peers in (
        (UP_ALL, up_all, G - 1), (ID_Y, id_y, Y - 1), (DOWN_IN, down_in, G - 1), (ID_G, id_g, G - 1),
        (UP_PICK, up_send, Y - 1), (DOWN_ALL, down_all, Y - 1), (OUT_SUM, out_sum, X - 1),
        (DOWN_PICK, down_send, G - 1), (TERM, term_send, G - 1), (IN_SUM, in_sum, X - 1),
        (TERM_Y, term_y_send, Y - 1), (UP_TERM, up_term_all, G - 1), (TERM_OWNER, term_owner_send, G - 1),
        (UP_TERM_Y, up_term_y_send, Y - 1),
    ):
        view = sent.at[pl.ds(0, peers)]
        pltpu.make_async_copy(view, view, send_sem.at[step]).wait()


def store_kernel(out_vm, grad_down_vm, grad_up_vm, out_hbm, grad_down_hbm, grad_up_hbm, sem):
    copies = [
        pltpu.make_async_copy(src, dst, sem.at[i])
        for i, (src, dst) in enumerate(
            ((out_vm, out_hbm), (grad_down_vm, grad_down_hbm), (grad_up_vm, grad_up_hbm))
        )
    ]
    for copy in copies:
        copy.start()
    for copy in copies:
        copy.wait()


def on_device(inputs, cotangent, frozen_key_weight, adapter_down_weight, adapter_up_weight, tenant_per_block):
    hbm = pl.BlockSpec(memory_space=pltpu.HBM)
    anywhere = pl.BlockSpec(memory_space=pl.ANY)
    vmem = pl.BlockSpec(memory_space=pltpu.VMEM)
    smem = pl.BlockSpec(memory_space=pltpu.SMEM)
    dma = pltpu.SemaphoreType.DMA
    results = (
        jax.ShapeDtypeStruct((ROWS, WIDTH), BF16),
        jax.ShapeDtypeStruct((1, RANK, WIDTH), F32),
        jax.ShapeDtypeStruct((1, RANK, KEYS), F32),
    )
    held = pl.pallas_call(
        kernel,
        out_shape=tuple(pltpu.VMEM(r.shape, r.dtype) for r in results),
        in_specs=[hbm] * 5 + [smem],
        out_specs=(vmem, vmem, vmem),
        scratch_shapes=[
            pltpu.VMEM((ROWS, WIDTH), BF16),
            pltpu.VMEM((ROWS, KEYS), BF16),
            pltpu.VMEM((X * WIDTH, KEYS), BF16),
            pltpu.VMEM((1, RANK, WIDTH), BF16),
            pltpu.VMEM((1, RANK, KEYS), BF16),
            pltpu.VMEM((X - 1, ROWS, WIDTH), BF16),
            pltpu.VMEM((ROWS, WIDTH), F32),
            pltpu.VMEM((X - 1, ROWS, WIDTH), BF16),
            pltpu.VMEM((2, HALF, WIDTH), BF16),
            pltpu.VMEM((1, 1, LANES), F32),
            pltpu.VMEM((G * RANK, Y * G * RANK), BF16),
            pltpu.VMEM((G, RANK, KEYS), BF16),
            pltpu.VMEM((Y, 1, LANES), F32),
            pltpu.VMEM((G, RANK, LANES), BF16),
            pltpu.VMEM((Y, G * RANK, LANES), BF16),
            pltpu.VMEM((G, 1, LANES), F32),
            pltpu.VMEM((Y, RANK, KEYS), BF16),
            pltpu.VMEM((Y, RANK, KEYS), BF16),
            pltpu.VMEM((X, RANK, ROWS), F32),
            pltpu.VMEM((G, RANK, LANES), BF16),
            pltpu.VMEM((G, RANK, LANES), BF16),
            pltpu.VMEM((X, RANK, ROWS), F32),
            pltpu.VMEM((G, RANK, LANES), BF16),
            pltpu.VMEM((G, RANK, LANES), BF16),
            pltpu.VMEM((Y, G * RANK, LANES), BF16),
            pltpu.VMEM((Y, G * RANK, LANES), BF16),
            pltpu.VMEM((G, RANK, LANES), F32),
            pltpu.VMEM((G, RANK, LANES), F32),
            pltpu.VMEM((RANK, KEYS), BF16),
            pltpu.VMEM((G, RANK, KEYS), BF16),
            pltpu.VMEM((Y, RANK, KEYS), F32),
            pltpu.VMEM((Y, RANK, KEYS), F32),
            dma((5,)), dma((STEPS,)), dma((STEPS,)), dma((8,)), dma((8,)),
        ],
        compiler_params=pltpu.CompilerParams(
            collective_id=0, has_side_effects=True, vmem_limit_bytes=60 << 20
        ),
    )(inputs, cotangent, frozen_key_weight, adapter_down_weight, adapter_up_weight, tenant_per_block)
    return pl.pallas_call(
        store_kernel,
        out_shape=results,
        in_specs=[anywhere] * 3,
        out_specs=(anywhere, anywhere, anywhere),
        scratch_shapes=[dma((3,))],
        compiler_params=pltpu.CompilerParams(vmem_limit_bytes=1 << 20),
    )(*held)


def solution(mesh):
    in_specs = (
        P("dp", "tensor"),
        P("dp", "tensor"),
        P(None, "tensor"),
        P("dp", None, "tensor"),
        P("dp", None, "tensor"),
        P("dp"),
    )
    out_specs = (P("dp", "tensor"), P("dp", None, "tensor"), P("dp", None, "tensor"))
    return jax.shard_map(
        on_device, mesh=mesh, in_specs=in_specs, out_specs=out_specs, check_vma=False
    )
```

```python
import jax
import jax.numpy as jnp
from jax import lax
from jax.experimental import pallas as pl
from jax.experimental.pallas import tpu as pltpu
from jax.sharding import PartitionSpec as P

MESH = pl.DeviceIdType.MESH
F32 = jnp.float32
BF16 = jnp.bfloat16
ADAPTER_SCALE = 2.0

Z, Y, CORES, X = 8, 4, 2, 4
G = Z * CORES
YC = Y * CORES
HALF_G = G // 2
ROWS, WIDTH, KEYS, RANK, LANES = 128, 2048, 256, 16, 128
HALF, FIRST, SECOND = 64, 32, 64

STEPS = 15
(
    UP_ALL, ID_Y, DOWN_IN, ID_G, UP_PICK, DOWN_ALL, OUT_SUM, DOWN_PICK, TERM, IN_SUM, TERM_FAR, TERM_NEAR, UP_TERM,
    TERM_OWNER, UP_TERM_Y,
) = range(STEPS)


def dot(a, b, dims=((1,), (0,))):
    return lax.dot_general(a, b, (dims, ((), ())), preferred_element_type=F32)


def kernel(
    inputs_hbm, cot_hbm, weight_hbm, down_hbm, up_hbm, tenant_ref,
    out_ref, grad_down_ref, grad_up_ref,
    xs, cot_vm, weight, down_vm, up_vm, partial, own, arrived, hop, ids, pick,
    up_all, id_y, down_in, down_all, id_g, up_send, up_recv, out_sum, down_send, down_recv, in_sum,
    term_send, term_recv, term_y_send, term_y_recv, term_owner_send, term_owner_recv,
    up_term, up_term_all, up_term_y_send, up_term_y_recv,
    load_sem, send_sem, recv_sem, xsend_sem, xrecv_sem,
):
    me, mx = lax.axis_index("dp"), lax.axis_index("tensor")
    z, y, c = lax.div(me, Y * CORES), lax.rem(lax.div(me, CORES), Y), lax.rem(me, CORES)
    g = z * CORES + c
    x_next, x_last = lax.rem(mx + 1, X), lax.rem(mx + X - 1, X)

    def group_member(i):
        h = lax.rem(g + G // 2 + (1 - 2 * lax.rem(i, 2)) * lax.div(i + 1, 2), G)
        return h, (lax.div(h, CORES) * Y + y) * CORES + lax.rem(h, CORES)

    def z_member(k):
        h = lax.rem(z + k, Z)
        return h, (h * Y + y) * CORES + c

    p = y * CORES + c

    def plane_member(k):
        h = lax.rem(p + k, YC)
        return h, z * YC + h

    def y_member(k):
        h = lax.rem(y + k, Y)
        return h, (z * Y + h) * CORES + c

    def send(step, src, dst, axis, device):
        pltpu.make_async_remote_copy(
            src, dst, send_sem.at[step], recv_sem.at[step], device_id={axis: device}, device_id_type=MESH
        ).start()

    def keep(step, src, dst):
        pltpu.make_async_copy(src, dst, recv_sem.at[step]).start()

    def received(step, dst):
        pltpu.make_async_copy(dst, dst, recv_sem.at[step]).wait()

    loads = [
        pltpu.make_async_copy(src, dst, load_sem.at[i])
        for i, (src, dst) in enumerate(
            ((up_hbm, up_vm), (down_hbm, down_vm), (cot_hbm, cot_vm), (weight_hbm, weight), (inputs_hbm, xs))
        )
    ]

    barrier = pltpu.get_barrier_semaphore()

    @pl.loop(0, G - 1)
    def _(i):
        _, device = group_member(i)
        pl.semaphore_signal(barrier, inc=1, device_id={"dp": device}, device_id_type=MESH)

    for k in (2, 1, 3):
        device = y_member(k)[1]
        pl.semaphore_signal(barrier, inc=1, device_id={"dp": device}, device_id_type=MESH)
        pl.semaphore_signal(barrier, inc=1, device_id={"dp": device + 1 - 2 * c}, device_id_type=MESH)
        pl.semaphore_signal(barrier, inc=1, device_id={"tensor": lax.rem(mx + k, X)}, device_id_type=MESH)

    for load in loads:
        load.start()
    ids[0] = jnp.full((1, LANES), tenant_ref[0], jnp.int32).astype(F32)
    loads[0].wait()
    loads[1].wait()
    for q in range(G):
        down_in[q] = down_vm[0, :, q * LANES : (q + 1) * LANES]
    pl.semaphore_wait(barrier, G - 1 + 2 * (Y - 1) + X - 1)

    my_rows = pl.ds(pl.multiple_of(g * RANK, RANK), RANK)

    @pl.loop(0, G - 1)
    def _(i):
        h, device = group_member(i)
        send(DOWN_IN, down_in.at[h], down_all.at[y, my_rows], "dp", device)

    keep(DOWN_IN, down_in.at[g], down_all.at[y, my_rows])

    for k in (4, 3, 5, 2, 6, 1, 7):
        send(UP_ALL, up_vm.at[0], up_all.at[z], "dp", z_member(k)[1])
    keep(UP_ALL, up_vm.at[0], up_all.at[z])
    for k in (4, 3, 5, 2, 6, 1, 7):
        send(ID_Y, ids.at[0], id_y.at[p], "dp", plane_member(k)[1])
    keep(ID_Y, ids.at[0], id_y.at[p])

    @pl.loop(0, G - 1)
    def _(i):
        send(ID_G, ids.at[0], id_g.at[g], "dp", group_member(i)[1])

    keep(ID_G, ids.at[0], id_g.at[g])

    def share(i, src, dst, device):
        return pltpu.make_async_remote_copy(
            src, dst, xsend_sem.at[i], xrecv_sem.at[i], device_id={"tensor": device}, device_id_type=MESH
        )

    low_half, high_half = pl.ds(0, HALF), pl.ds(HALF, ROWS - HALF)
    first, second = pl.ds(0, FIRST), pl.ds(FIRST, SECOND)
    rest = pl.ds(FIRST + SECOND, ROWS - FIRST - SECOND)
    hops = (
        share(0, partial.at[1, low_half], hop.at[0], x_next),
        share(1, partial.at[1, high_half], hop.at[1], x_last),
    )
    nearby = [
        (
            share(2 * i + 2, partial.at[0, part], arrived.at[0, part], x_next),
            share(2 * i + 3, partial.at[2, part], arrived.at[2, part], x_last),
        )
        for i, part in enumerate((first, second, rest))
    ]
    relayed = (
        share(8, hop.at[0], arrived.at[1, low_half], x_next),
        share(9, hop.at[1], arrived.at[1, high_half], x_last),
    )
    loads[2].wait()
    cot = cot_vm[...]
    loads[3].wait()
    for k in (2, 1, 3, 0):
        at = pl.multiple_of(lax.rem(mx + k, X) * WIDTH, WIDTH)
        product = dot(cot, weight[pl.ds(at, WIDTH), :], ((1,), (1,)))
        if k == 0:
            own[...] = product
        else:
            partial[k - 1] = product.astype(BF16)
        if k == 2:
            for copy in hops:
                copy.start()
        if k == 3:
            for copy in nearby[0]:
                copy.start()

    def place(t):
        t = t.astype(jnp.int32)
        return t >> 3, (t >> 1) & 3, t & 1

    rank = lax.broadcasted_iota(jnp.int32, (RANK, 1), 0)
    slot = lax.broadcasted_iota(jnp.int32, (RANK, Z * RANK), 1)
    received(ID_Y, id_y)
    wanted = []
    for h in range(YC):
        t_z, t_y, t_c = place(jnp.broadcast_to(id_y[h, :, :1], (RANK, 1)))
        wanted.append((slot == jnp.where(t_y * CORES + t_c == p, t_z * RANK + rank, -1)).astype(F32).astype(BF16))
    wanted = jnp.concatenate(wanted, axis=0)
    received(UP_ALL, up_all)
    chosen = dot(wanted, up_all[...].reshape(Z * RANK, KEYS)).astype(BF16)
    for h in range(YC):
        up_send[h] = chosen[h * RANK : (h + 1) * RANK]
    for k in (4, 3, 5, 2, 6, 1, 7):
        h, device = plane_member(k)
        send(UP_PICK, up_send.at[h], up_recv.at[p], "dp", device)
    keep(UP_PICK, up_send.at[p], up_recv.at[p])

    received(DOWN_IN, down_all.at[y])
    for k in (2, 1, 3):
        send(DOWN_ALL, down_all.at[y], down_all.at[y], "dp", y_member(k)[1])

    received(ID_G, id_g)
    slot = lax.broadcasted_iota(jnp.int32, (RANK, Y * G * RANK), 1)
    for h in range(G):
        t_z, t_y, t_c = place(jnp.broadcast_to(id_g[h, :, :1], (RANK, 1)))
        t_slot = t_y * G + t_z * CORES + t_c
        pick[h * RANK : (h + 1) * RANK, :] = (slot == t_slot * RANK + rank).astype(F32).astype(BF16)
    slot = lax.broadcasted_iota(jnp.int32, (RANK, YC * RANK), 1)
    mine = []
    for h in range(Z):
        t_z, t_y, t_c = place(jnp.broadcast_to(id_g[h * CORES + c, :, :1], (RANK, 1)))
        mine.append((slot == jnp.where(t_z == z, (t_y * CORES + t_c) * RANK + rank, -1)).astype(F32).astype(BF16))
    mine = jnp.concatenate(mine, axis=0)

    def pick_of(q):
        return pick[:, q * G * RANK : (q + 1) * G * RANK]

    received(UP_PICK, up_recv)
    up_b = up_recv[0].astype(F32)
    for h in range(1, YC):
        up_b += up_recv[h].astype(F32)
    out_sum[mx] = ADAPTER_SCALE * dot(up_b.astype(BF16), cot, ((1,), (1,)))
    for k in (2, 1, 3):
        send(OUT_SUM, out_sum.at[mx], out_sum.at[mx], "tensor", lax.rem(mx + k, X))
    for copy in nearby[1]:
        copy.start()

    received(DOWN_ALL, down_all.at[pl.ds(0, Y - 1)])
    tiles = jnp.zeros((G * RANK, LANES), F32)
    for q in range(Y):
        tiles += dot(pick_of(q), down_all[q])
    for h in range(G):
        down_send[h] = tiles[h * RANK : (h + 1) * RANK].astype(BF16)

    @pl.loop(0, G - 1)
    def _(i):
        h, device = group_member(i)
        send(DOWN_PICK, down_send.at[h], down_recv.at[g], "dp", device)

    keep(DOWN_PICK, down_send.at[g], down_recv.at[g])

    loads[4].wait()
    received(OUT_SUM, out_sum.at[pl.ds(0, X - 1)])
    low_out = ((out_sum[0] + out_sum[1]) + (out_sum[2] + out_sum[3])).astype(BF16)
    term = dot(low_out, xs[...]).astype(BF16)
    for h in range(G):
        term_send[h] = term[:, h * LANES : (h + 1) * LANES]

    @pl.loop(0, G - 1)
    def _(i):
        h, device = group_member(i)
        send(TERM, term_send.at[h], term_recv.at[g], "dp", device)

    keep(TERM, term_send.at[g], term_recv.at[g])

    received(DOWN_PICK, down_recv)
    down_b = jnp.concatenate([down_recv[h] for h in range(G)], axis=1)
    in_sum[mx] = dot(down_b, xs[...], ((1,), (1,)))
    for k in (2, 1, 3):
        send(IN_SUM, in_sum.at[mx], in_sum.at[mx], "tensor", lax.rem(mx + k, X))
    for copy in hops:
        copy.wait_recv()
    for copy in relayed + nearby[2]:
        copy.start()
    own[...] += dot(low_out, down_b, ((0,), (0,)))

    received(TERM, term_recv)
    terms = term_recv[...].reshape(G * RANK, LANES)
    for q in range(Y):
        sums = dot(pick_of(q), terms, ((0,), (0,))).astype(BF16)
        for h in range(G):
            term_y_send[q, lax.rem(h - g + G + G - 4, G)] = sums[h * RANK : (h + 1) * RANK]
    halves = ((TERM_FAR, pl.ds(0, HALF_G)), (TERM_NEAR, pl.ds(HALF_G, HALF_G)))
    for step, half in halves:
        for k in (2, 1, 3):
            h, device = y_member(k)
            send(step, term_y_send.at[h, half], term_y_recv.at[y, half], "dp", device)
        keep(step, term_y_send.at[y, half], term_y_recv.at[y, half])

    received(IN_SUM, in_sum.at[pl.ds(0, X - 1)])
    low_in = ((in_sum[0] + in_sum[1]) + (in_sum[2] + in_sum[3])).astype(BF16)
    up_term[...] = (ADAPTER_SCALE * dot(low_in, cot)).astype(BF16)

    for k in (4, 3, 5, 2, 6, 1, 7):
        send(UP_TERM, up_term, up_term_all.at[z], "dp", z_member(k)[1])
    keep(UP_TERM, up_term, up_term_all.at[z])

    for step, half in halves:
        received(step, term_y_recv.at[pl.ds(0, Y), half])
        for j in range(half.start, half.start + HALF_G):
            term_owner_send[j] = (term_y_recv[0, j].astype(F32) + term_y_recv[1, j].astype(F32)) + (
                term_y_recv[2, j].astype(F32) + term_y_recv[3, j].astype(F32)
            )
        for j in (4, 3, 5, 2, 6, 1, 7, 0):
            place_j = half.start + j
            h = lax.rem(g + 4 + place_j, G)
            if place_j == G - 4:
                keep(TERM_OWNER, term_owner_send.at[place_j], term_owner_recv.at[g])
            else:
                device = (lax.div(h, CORES) * Y + y) * CORES + lax.rem(h, CORES)
                send(TERM_OWNER, term_owner_send.at[place_j], term_owner_recv.at[g], "dp", device)

    received(UP_TERM, up_term_all)
    sums = dot(mine, up_term_all[...].reshape(Z * RANK, KEYS), ((0,), (0,)))
    for h in range(YC):
        up_term_y_send[h] = sums[h * RANK : (h + 1) * RANK]
    for k in (4, 3, 5, 2, 6, 1, 7):
        h, device = plane_member(k)
        send(UP_TERM_Y, up_term_y_send.at[h], up_term_y_recv.at[p], "dp", device)
    keep(UP_TERM_Y, up_term_y_send.at[p], up_term_y_recv.at[p])

    shares = nearby[0] + nearby[1] + nearby[2] + relayed
    for copy in shares:
        copy.wait_recv()
    for i in range(WIDTH // KEYS):
        columns = slice(i * KEYS, (i + 1) * KEYS)
        total = own[:, columns]
        for k in range(X - 1):
            total += arrived[k, :, columns].astype(F32)
        out_ref[:, columns] = total.astype(BF16)
    received(TERM_OWNER, term_owner_recv)
    for h in range(G):
        grad_down_ref[0, :, h * LANES : (h + 1) * LANES] = term_owner_recv[h]
    received(UP_TERM_Y, up_term_y_recv)
    total = up_term_y_recv[0]
    for h in range(1, YC):
        total += up_term_y_recv[h]
    grad_up_ref[0] = total

    for copy in hops + shares:
        copy.wait_send()
    for step, sent, peers in (
        (UP_ALL, up_all, Z - 1), (ID_Y, id_y, YC - 1), (DOWN_IN, down_in, G - 1), (ID_G, id_g, G - 1),
        (UP_PICK, up_send, YC - 1), (DOWN_ALL, down_all, Y - 1), (OUT_SUM, out_sum, X - 1),
        (DOWN_PICK, down_send, G - 1), (TERM, term_send, G - 1), (IN_SUM, in_sum, X - 1),
        (UP_TERM, up_term_all, Z - 1), (TERM_OWNER, term_owner_send, G - 1), (UP_TERM_Y, up_term_y_send, YC - 1),
    ):
        view = sent.at[pl.ds(0, peers)]
        pltpu.make_async_copy(view, view, send_sem.at[step]).wait()
    for step, half in halves:
        view = term_y_send.at[pl.ds(0, Y - 1), half]
        pltpu.make_async_copy(view, view, send_sem.at[step]).wait()


def store_kernel(out_vm, grad_down_vm, grad_up_vm, out_hbm, grad_down_hbm, grad_up_hbm, sem):
    copies = [
        pltpu.make_async_copy(src, dst, sem.at[i])
        for i, (src, dst) in enumerate(
            ((out_vm, out_hbm), (grad_down_vm, grad_down_hbm), (grad_up_vm, grad_up_hbm))
        )
    ]
    for copy in copies:
        copy.start()
    for copy in copies:
        copy.wait()


def on_device(inputs, cotangent, frozen_key_weight, adapter_down_weight, adapter_up_weight, tenant_per_block):
    hbm = pl.BlockSpec(memory_space=pltpu.HBM)
    anywhere = pl.BlockSpec(memory_space=pl.ANY)
    vmem = pl.BlockSpec(memory_space=pltpu.VMEM)
    smem = pl.BlockSpec(memory_space=pltpu.SMEM)
    dma = pltpu.SemaphoreType.DMA
    results = (
        jax.ShapeDtypeStruct((ROWS, WIDTH), BF16),
        jax.ShapeDtypeStruct((1, RANK, WIDTH), F32),
        jax.ShapeDtypeStruct((1, RANK, KEYS), F32),
    )
    held = pl.pallas_call(
        kernel,
        out_shape=tuple(pltpu.VMEM(r.shape, r.dtype) for r in results),
        in_specs=[hbm] * 5 + [smem],
        out_specs=(vmem, vmem, vmem),
        scratch_shapes=[
            pltpu.VMEM((ROWS, WIDTH), BF16),
            pltpu.VMEM((ROWS, KEYS), BF16),
            pltpu.VMEM((X * WIDTH, KEYS), BF16),
            pltpu.VMEM((1, RANK, WIDTH), BF16),
            pltpu.VMEM((1, RANK, KEYS), BF16),
            pltpu.VMEM((X - 1, ROWS, WIDTH), BF16),
            pltpu.VMEM((ROWS, WIDTH), F32),
            pltpu.VMEM((X - 1, ROWS, WIDTH), BF16),
            pltpu.VMEM((2, HALF, WIDTH), BF16),
            pltpu.VMEM((1, 1, LANES), F32),
            pltpu.VMEM((G * RANK, Y * G * RANK), BF16),
            pltpu.VMEM((Z, RANK, KEYS), BF16),
            pltpu.VMEM((YC, 1, LANES), F32),
            pltpu.VMEM((G, RANK, LANES), BF16),
            pltpu.VMEM((Y, G * RANK, LANES), BF16),
            pltpu.VMEM((G, 1, LANES), F32),
            pltpu.VMEM((YC, RANK, KEYS), BF16),
            pltpu.VMEM((YC, RANK, KEYS), BF16),
            pltpu.VMEM((X, RANK, ROWS), F32),
            pltpu.VMEM((G, RANK, LANES), BF16),
            pltpu.VMEM((G, RANK, LANES), BF16),
            pltpu.VMEM((X, RANK, ROWS), F32),
            pltpu.VMEM((G, RANK, LANES), BF16),
            pltpu.VMEM((G, RANK, LANES), BF16),
            pltpu.VMEM((Y, G, RANK, LANES), BF16),
            pltpu.VMEM((Y, G, RANK, LANES), BF16),
            pltpu.VMEM((G, RANK, LANES), F32),
            pltpu.VMEM((G, RANK, LANES), F32),
            pltpu.VMEM((RANK, KEYS), BF16),
            pltpu.VMEM((Z, RANK, KEYS), BF16),
            pltpu.VMEM((YC, RANK, KEYS), F32),
            pltpu.VMEM((YC, RANK, KEYS), F32),
            dma((5,)), dma((STEPS,)), dma((STEPS,)), dma((10,)), dma((10,)),
        ],
        compiler_params=pltpu.CompilerParams(
            collective_id=0, has_side_effects=True, vmem_limit_bytes=60 << 20
        ),
    )(inputs, cotangent, frozen_key_weight, adapter_down_weight, adapter_up_weight, tenant_per_block)
    return pl.pallas_call(
        store_kernel,
        out_shape=results,
        in_specs=[anywhere] * 3,
        out_specs=(anywhere, anywhere, anywhere),
        scratch_shapes=[dma((3,))],
        compiler_params=pltpu.CompilerParams(vmem_limit_bytes=1 << 20),
    )(*held)


def solution(mesh):
    in_specs = (
        P("dp", "tensor"),
        P("dp", "tensor"),
        P(None, "tensor"),
        P("dp", None, "tensor"),
        P("dp", None, "tensor"),
        P("dp"),
    )
    out_specs = (P("dp", "tensor"), P("dp", None, "tensor"), P("dp", None, "tensor"))
    return jax.shard_map(
        on_device, mesh=mesh, in_specs=in_specs, out_specs=out_specs, check_vma=False
    )
```

```python
import jax
import jax.numpy as jnp
from jax import lax
from jax.experimental import pallas as pl
from jax.experimental.pallas import tpu as pltpu
from jax.sharding import PartitionSpec as P

MESH = pl.DeviceIdType.MESH
F32 = jnp.float32
BF16 = jnp.bfloat16
ADAPTER_SCALE = 2.0

Z, Y, CORES, X = 8, 4, 2, 4
G = Z * CORES
YC = Y * CORES
HALF_G = G // 2
ROWS, WIDTH, KEYS, RANK, LANES = 128, 2048, 256, 16, 128
HALF, FIRST, SECOND = 64, 32, 64

STEPS = 15
(
    UP_ALL, ID_Y, DOWN_IN, ID_G, UP_PICK, DOWN_ALL, OUT_SUM, DOWN_PICK, TERM, IN_SUM, TERM_FAR, TERM_NEAR, UP_TERM,
    TERM_OWNER, UP_TERM_Y,
) = range(STEPS)


def dot(a, b, dims=((1,), (0,))):
    return lax.dot_general(a, b, (dims, ((), ())), preferred_element_type=F32)


def kernel(
    inputs_hbm, cot_hbm, weight_hbm, down_hbm, up_hbm, tenant_ref,
    out_ref, grad_down_ref, grad_up_ref,
    xs, cot_vm, weight, down_vm, up_vm, partial, own, arrived, hop, ids, pick,
    up_all, id_y, down_in, down_all, id_g, up_send, up_recv, out_sum, down_send, down_recv, in_sum,
    term_send, term_recv, term_y_send, term_y_recv, term_owner_send, term_owner_recv,
    up_term, up_term_all, up_term_y_send, up_term_y_recv,
    load_sem, send_sem, recv_sem, xsend_sem, xrecv_sem,
):
    me, mx = lax.axis_index("dp"), lax.axis_index("tensor")
    z, y, c = lax.div(me, Y * CORES), lax.rem(lax.div(me, CORES), Y), lax.rem(me, CORES)
    g = z * CORES + c
    x_next, x_last = lax.rem(mx + 1, X), lax.rem(mx + X - 1, X)

    def group_member(i):
        h = lax.rem(g + G // 2 + (1 - 2 * lax.rem(i, 2)) * lax.div(i + 1, 2), G)
        return h, (lax.div(h, CORES) * Y + y) * CORES + lax.rem(h, CORES)

    def z_member(k):
        h = lax.rem(z + k, Z)
        return h, (h * Y + y) * CORES + c

    p = y * CORES + c

    def plane_member(k):
        h = lax.rem(p + k, YC)
        return h, z * YC + h

    def y_member(k):
        h = lax.rem(y + k, Y)
        return h, (z * Y + h) * CORES + c

    def send(step, src, dst, axis, device):
        pltpu.make_async_remote_copy(
            src, dst, send_sem.at[step], recv_sem.at[step], device_id={axis: device}, device_id_type=MESH
        ).start()

    def keep(step, src, dst):
        pltpu.make_async_copy(src, dst, recv_sem.at[step]).start()

    def received(step, dst):
        pltpu.make_async_copy(dst, dst, recv_sem.at[step]).wait()

    loads = [
        pltpu.make_async_copy(src, dst, load_sem.at[i])
        for i, (src, dst) in enumerate(
            ((up_hbm, up_vm), (down_hbm, down_vm), (cot_hbm, cot_vm), (weight_hbm, weight), (inputs_hbm, xs))
        )
    ]

    barrier = pltpu.get_barrier_semaphore()

    @pl.loop(0, G - 1)
    def _(i):
        _, device = group_member(i)
        pl.semaphore_signal(barrier, inc=1, device_id={"dp": device}, device_id_type=MESH)

    for k in (2, 1, 3):
        device = y_member(k)[1]
        pl.semaphore_signal(barrier, inc=1, device_id={"dp": device}, device_id_type=MESH)
        pl.semaphore_signal(barrier, inc=1, device_id={"dp": device + 1 - 2 * c}, device_id_type=MESH)
        pl.semaphore_signal(barrier, inc=1, device_id={"tensor": lax.rem(mx + k, X)}, device_id_type=MESH)

    for load in loads:
        load.start()
    ids[0] = jnp.full((1, LANES), tenant_ref[0], jnp.int32).astype(F32)
    loads[0].wait()
    loads[1].wait()
    for q in range(G):
        down_in[q] = down_vm[0, :, q * LANES : (q + 1) * LANES]
    pl.semaphore_wait(barrier, G - 1 + 2 * (Y - 1) + X - 1)

    my_rows = pl.ds(pl.multiple_of(g * RANK, RANK), RANK)

    @pl.loop(0, G - 1)
    def _(i):
        h, device = group_member(i)
        send(DOWN_IN, down_in.at[h], down_all.at[y, my_rows], "dp", device)

    keep(DOWN_IN, down_in.at[g], down_all.at[y, my_rows])

    for k in (4, 3, 5, 2, 6, 1, 7):
        send(UP_ALL, up_vm.at[0], up_all.at[z], "dp", z_member(k)[1])
    keep(UP_ALL, up_vm.at[0], up_all.at[z])
    for k in (4, 3, 5, 2, 6, 1, 7):
        send(ID_Y, ids.at[0], id_y.at[p], "dp", plane_member(k)[1])
    keep(ID_Y, ids.at[0], id_y.at[p])

    @pl.loop(0, G - 1)
    def _(i):
        send(ID_G, ids.at[0], id_g.at[g], "dp", group_member(i)[1])

    keep(ID_G, ids.at[0], id_g.at[g])

    def share(i, src, dst, device):
        return pltpu.make_async_remote_copy(
            src, dst, xsend_sem.at[i], xrecv_sem.at[i], device_id={"tensor": device}, device_id_type=MESH
        )

    low_half, high_half = pl.ds(0, HALF), pl.ds(HALF, ROWS - HALF)
    first, second = pl.ds(0, FIRST), pl.ds(FIRST, SECOND)
    rest = pl.ds(FIRST + SECOND, ROWS - FIRST - SECOND)
    hops = (
        share(0, partial.at[1, low_half], hop.at[0], x_next),
        share(1, partial.at[1, high_half], hop.at[1], x_last),
    )
    nearby = [
        (
            share(2 * i + 2, partial.at[0, part], arrived.at[0, part], x_next),
            share(2 * i + 3, partial.at[2, part], arrived.at[2, part], x_last),
        )
        for i, part in enumerate((first, second, rest))
    ]
    relayed = (
        share(8, hop.at[0], arrived.at[1, low_half], x_next),
        share(9, hop.at[1], arrived.at[1, high_half], x_last),
    )
    loads[2].wait()
    cot = cot_vm[...]
    loads[3].wait()
    for k in (2, 1, 3, 0):
        at = pl.multiple_of(lax.rem(mx + k, X) * WIDTH, WIDTH)
        product = dot(cot, weight[pl.ds(at, WIDTH), :], ((1,), (1,)))
        if k == 0:
            own[...] = product
        else:
            partial[k - 1] = product.astype(BF16)
        if k == 2:
            for copy in hops:
                copy.start()
        if k == 3:
            for copy in nearby[0]:
                copy.start()

    def place(t):
        t = t.astype(jnp.int32)
        return t >> 3, (t >> 1) & 3, t & 1

    rank = lax.broadcasted_iota(jnp.int32, (RANK, 1), 0)
    slot = lax.broadcasted_iota(jnp.int32, (RANK, Z * RANK), 1)
    received(ID_Y, id_y)
    wanted = []
    for h in range(YC):
        t_z, t_y, t_c = place(jnp.broadcast_to(id_y[h, :, :1], (RANK, 1)))
        wanted.append((slot == jnp.where(t_y * CORES + t_c == p, t_z * RANK + rank, -1)).astype(F32).astype(BF16))
    wanted = jnp.concatenate(wanted, axis=0)
    received(UP_ALL, up_all)
    chosen = dot(wanted, up_all[...].reshape(Z * RANK, KEYS)).astype(BF16)
    for h in range(YC):
        up_send[h] = chosen[h * RANK : (h + 1) * RANK]
    for k in (4, 3, 5, 2, 6, 1, 7):
        h, device = plane_member(k)
        send(UP_PICK, up_send.at[h], up_recv.at[p], "dp", device)
    keep(UP_PICK, up_send.at[p], up_recv.at[p])

    received(DOWN_IN, down_all.at[y])
    for k in (2, 1, 3):
        send(DOWN_ALL, down_all.at[y], down_all.at[y], "dp", y_member(k)[1])

    received(ID_G, id_g)
    slot = lax.broadcasted_iota(jnp.int32, (RANK, Y * G * RANK), 1)
    for h in range(G):
        t_z, t_y, t_c = place(jnp.broadcast_to(id_g[h, :, :1], (RANK, 1)))
        t_slot = t_y * G + t_z * CORES + t_c
        pick[h * RANK : (h + 1) * RANK, :] = (slot == t_slot * RANK + rank).astype(F32).astype(BF16)
    slot = lax.broadcasted_iota(jnp.int32, (RANK, Y * RANK), 1)
    mine = []
    for h in range(G):
        t_z, t_y, t_c = place(jnp.broadcast_to(id_g[h, :, :1], (RANK, 1)))
        mine.append((slot == jnp.where(t_z * CORES + t_c == g, t_y * RANK + rank, -1)).astype(F32).astype(BF16))
    mine = jnp.concatenate(mine, axis=0)

    def pick_of(q):
        return pick[:, q * G * RANK : (q + 1) * G * RANK]

    received(UP_PICK, up_recv)
    up_b = up_recv[0].astype(F32)
    for h in range(1, YC):
        up_b += up_recv[h].astype(F32)
    out_sum[mx] = ADAPTER_SCALE * dot(up_b.astype(BF16), cot, ((1,), (1,)))
    for k in (2, 1, 3):
        send(OUT_SUM, out_sum.at[mx], out_sum.at[mx], "tensor", lax.rem(mx + k, X))
    for copy in nearby[1]:
        copy.start()

    received(DOWN_ALL, down_all.at[pl.ds(0, Y - 1)])
    tiles = jnp.zeros((G * RANK, LANES), F32)
    for q in range(Y):
        tiles += dot(pick_of(q), down_all[q])
    for h in range(G):
        down_send[h] = tiles[h * RANK : (h + 1) * RANK].astype(BF16)

    @pl.loop(0, G - 1)
    def _(i):
        h, device = group_member(i)
        send(DOWN_PICK, down_send.at[h], down_recv.at[g], "dp", device)

    keep(DOWN_PICK, down_send.at[g], down_recv.at[g])

    loads[4].wait()
    received(OUT_SUM, out_sum.at[pl.ds(0, X - 1)])
    low_out = ((out_sum[0] + out_sum[1]) + (out_sum[2] + out_sum[3])).astype(BF16)
    term = dot(low_out, xs[...]).astype(BF16)
    for h in range(G):
        term_send[h] = term[:, h * LANES : (h + 1) * LANES]

    @pl.loop(0, G - 1)
    def _(i):
        h, device = group_member(i)
        send(TERM, term_send.at[h], term_recv.at[g], "dp", device)

    keep(TERM, term_send.at[g], term_recv.at[g])

    received(DOWN_PICK, down_recv)
    down_b = jnp.concatenate([down_recv[h] for h in range(G)], axis=1)
    in_sum[mx] = dot(down_b, xs[...], ((1,), (1,)))
    for k in (2, 1, 3):
        send(IN_SUM, in_sum.at[mx], in_sum.at[mx], "tensor", lax.rem(mx + k, X))
    for copy in hops:
        copy.wait_recv()
    for copy in relayed + nearby[2]:
        copy.start()
    own[...] += dot(low_out, down_b, ((0,), (0,)))

    received(TERM, term_recv)
    terms = term_recv[...].reshape(G * RANK, LANES)
    for q in range(Y):
        sums = dot(pick_of(q), terms, ((0,), (0,))).astype(BF16)
        for h in range(G):
            term_y_send[q, lax.rem(h - g + G + G - 4, G)] = sums[h * RANK : (h + 1) * RANK]
    halves = ((TERM_FAR, pl.ds(0, HALF_G)), (TERM_NEAR, pl.ds(HALF_G, HALF_G)))
    for step, half in halves:
        for k in (2, 1, 3):
            h, device = y_member(k)
            send(step, term_y_send.at[h, half], term_y_recv.at[y, half], "dp", device)
        keep(step, term_y_send.at[y, half], term_y_recv.at[y, half])

    received(IN_SUM, in_sum.at[pl.ds(0, X - 1)])
    low_in = ((in_sum[0] + in_sum[1]) + (in_sum[2] + in_sum[3])).astype(BF16)
    up_term[...] = (ADAPTER_SCALE * dot(low_in, cot)).astype(BF16)

    @pl.loop(0, G - 1)
    def _(i):
        send(UP_TERM, up_term, up_term_all.at[g], "dp", group_member(i)[1])

    keep(UP_TERM, up_term, up_term_all.at[g])

    for step, half in halves:
        received(step, term_y_recv.at[pl.ds(0, Y), half])
        for j in range(half.start, half.start + HALF_G):
            term_owner_send[j] = (term_y_recv[0, j].astype(F32) + term_y_recv[1, j].astype(F32)) + (
                term_y_recv[2, j].astype(F32) + term_y_recv[3, j].astype(F32)
            )
        for j in (4, 3, 5, 2, 6, 1, 7, 0):
            place_j = half.start + j
            h = lax.rem(g + 4 + place_j, G)
            if place_j == G - 4:
                keep(TERM_OWNER, term_owner_send.at[place_j], term_owner_recv.at[g])
            else:
                device = (lax.div(h, CORES) * Y + y) * CORES + lax.rem(h, CORES)
                send(TERM_OWNER, term_owner_send.at[place_j], term_owner_recv.at[g], "dp", device)

    received(UP_TERM, up_term_all)
    sums = dot(mine, up_term_all[...].reshape(G * RANK, KEYS), ((0,), (0,)))
    for h in range(Y):
        up_term_y_send[h] = sums[h * RANK : (h + 1) * RANK]
    for k in (2, 1, 3):
        h, device = y_member(k)
        send(UP_TERM_Y, up_term_y_send.at[h], up_term_y_recv.at[y], "dp", device)
    keep(UP_TERM_Y, up_term_y_send.at[y], up_term_y_recv.at[y])

    shares = nearby[0] + nearby[1] + nearby[2] + relayed
    for copy in shares:
        copy.wait_recv()
    for i in range(WIDTH // KEYS):
        columns = slice(i * KEYS, (i + 1) * KEYS)
        total = own[:, columns]
        for k in range(X - 1):
            total += arrived[k, :, columns].astype(F32)
        out_ref[:, columns] = total.astype(BF16)
    received(TERM_OWNER, term_owner_recv)
    for h in range(G):
        grad_down_ref[0, :, h * LANES : (h + 1) * LANES] = term_owner_recv[h]
    received(UP_TERM_Y, up_term_y_recv)
    grad_up_ref[0] = (up_term_y_recv[0] + up_term_y_recv[1]) + (up_term_y_recv[2] + up_term_y_recv[3])

    for copy in hops + shares:
        copy.wait_send()
    for step, sent, peers in (
        (UP_ALL, up_all, Z - 1), (ID_Y, id_y, YC - 1), (DOWN_IN, down_in, G - 1), (ID_G, id_g, G - 1),
        (UP_PICK, up_send, YC - 1), (DOWN_ALL, down_all, Y - 1), (OUT_SUM, out_sum, X - 1),
        (DOWN_PICK, down_send, G - 1), (TERM, term_send, G - 1), (IN_SUM, in_sum, X - 1),
        (UP_TERM, up_term_all, G - 1), (TERM_OWNER, term_owner_send, G - 1), (UP_TERM_Y, up_term_y_send, Y - 1),
    ):
        view = sent.at[pl.ds(0, peers)]
        pltpu.make_async_copy(view, view, send_sem.at[step]).wait()
    for step, half in halves:
        view = term_y_send.at[pl.ds(0, Y - 1), half]
        pltpu.make_async_copy(view, view, send_sem.at[step]).wait()


def store_kernel(out_vm, grad_down_vm, grad_up_vm, out_hbm, grad_down_hbm, grad_up_hbm, sem):
    copies = [
        pltpu.make_async_copy(src, dst, sem.at[i])
        for i, (src, dst) in enumerate(
            ((out_vm, out_hbm), (grad_down_vm, grad_down_hbm), (grad_up_vm, grad_up_hbm))
        )
    ]
    for copy in copies:
        copy.start()
    for copy in copies:
        copy.wait()


def on_device(inputs, cotangent, frozen_key_weight, adapter_down_weight, adapter_up_weight, tenant_per_block):
    hbm = pl.BlockSpec(memory_space=pltpu.HBM)
    anywhere = pl.BlockSpec(memory_space=pl.ANY)
    vmem = pl.BlockSpec(memory_space=pltpu.VMEM)
    smem = pl.BlockSpec(memory_space=pltpu.SMEM)
    dma = pltpu.SemaphoreType.DMA
    results = (
        jax.ShapeDtypeStruct((ROWS, WIDTH), BF16),
        jax.ShapeDtypeStruct((1, RANK, WIDTH), F32),
        jax.ShapeDtypeStruct((1, RANK, KEYS), F32),
    )
    held = pl.pallas_call(
        kernel,
        out_shape=tuple(pltpu.VMEM(r.shape, r.dtype) for r in results),
        in_specs=[hbm] * 5 + [smem],
        out_specs=(vmem, vmem, vmem),
        scratch_shapes=[
            pltpu.VMEM((ROWS, WIDTH), BF16),
            pltpu.VMEM((ROWS, KEYS), BF16),
            pltpu.VMEM((X * WIDTH, KEYS), BF16),
            pltpu.VMEM((1, RANK, WIDTH), BF16),
            pltpu.VMEM((1, RANK, KEYS), BF16),
            pltpu.VMEM((X - 1, ROWS, WIDTH), BF16),
            pltpu.VMEM((ROWS, WIDTH), F32),
            pltpu.VMEM((X - 1, ROWS, WIDTH), BF16),
            pltpu.VMEM((2, HALF, WIDTH), BF16),
            pltpu.VMEM((1, 1, LANES), F32),
            pltpu.VMEM((G * RANK, Y * G * RANK), BF16),
            pltpu.VMEM((Z, RANK, KEYS), BF16),
            pltpu.VMEM((YC, 1, LANES), F32),
            pltpu.VMEM((G, RANK, LANES), BF16),
            pltpu.VMEM((Y, G * RANK, LANES), BF16),
            pltpu.VMEM((G, 1, LANES), F32),
            pltpu.VMEM((YC, RANK, KEYS), BF16),
            pltpu.VMEM((YC, RANK, KEYS), BF16),
            pltpu.VMEM((X, RANK, ROWS), F32),
            pltpu.VMEM((G, RANK, LANES), BF16),
            pltpu.VMEM((G, RANK, LANES), BF16),
            pltpu.VMEM((X, RANK, ROWS), F32),
            pltpu.VMEM((G, RANK, LANES), BF16),
            pltpu.VMEM((G, RANK, LANES), BF16),
            pltpu.VMEM((Y, G, RANK, LANES), BF16),
            pltpu.VMEM((Y, G, RANK, LANES), BF16),
            pltpu.VMEM((G, RANK, LANES), F32),
            pltpu.VMEM((G, RANK, LANES), F32),
            pltpu.VMEM((RANK, KEYS), BF16),
            pltpu.VMEM((G, RANK, KEYS), BF16),
            pltpu.VMEM((Y, RANK, KEYS), F32),
            pltpu.VMEM((Y, RANK, KEYS), F32),
            dma((5,)), dma((STEPS,)), dma((STEPS,)), dma((10,)), dma((10,)),
        ],
        compiler_params=pltpu.CompilerParams(
            collective_id=0, has_side_effects=True, vmem_limit_bytes=60 << 20
        ),
    )(inputs, cotangent, frozen_key_weight, adapter_down_weight, adapter_up_weight, tenant_per_block)
    return pl.pallas_call(
        store_kernel,
        out_shape=results,
        in_specs=[anywhere] * 3,
        out_specs=(anywhere, anywhere, anywhere),
        scratch_shapes=[dma((3,))],
        compiler_params=pltpu.CompilerParams(vmem_limit_bytes=1 << 20),
    )(*held)


def solution(mesh):
    in_specs = (
        P("dp", "tensor"),
        P("dp", "tensor"),
        P(None, "tensor"),
        P("dp", None, "tensor"),
        P("dp", None, "tensor"),
        P("dp"),
    )
    out_specs = (P("dp", "tensor"), P("dp", None, "tensor"), P("dp", None, "tensor"))
    return jax.shard_map(
        on_device, mesh=mesh, in_specs=in_specs, out_specs=out_specs, check_vma=False
    )
```
